128 devices in a mesh: ctx: 64 (over z, x, y), head: 2 (over core).
Axes of the slice: x: 4, y: 4, z: 4, core: 2. Of those that a mesh axis runs over, the one named last changes fastest.
Arguments:
- query_rows: bfloat16 [65536, 2048], P('ctx', 'head'), may hold values from -6 to 6
- key_rows: bfloat16 [65536, 2048], P('ctx', 'head'), may hold values from -6 to 6
- value_rows: bfloat16 [65536, 2048], P('ctx', 'head'), may hold values from -6 to 6
- out_grad: bfloat16 [65536, 2048], P('ctx', 'head'), may hold values from -6 to 6
- out_weight: bfloat16 [2048, 2048], P('head'), may hold values from -0.125 to 0.125
Outputs:
- query_gradient: bfloat16 [65536, 2048], P('ctx', 'head')
- key_gradient: bfloat16 [65536, 2048], P('ctx', 'head')
- value_gradient: bfloat16 [65536, 2048], P('ctx', 'head')
The draws below stay inside these ranges and needn't reach their ends.
All inputs are finite; a program needn't handle non-finite values.
Results may differ from the reference program's by a relative error of at most 0.005.
Values may be sent and summed in bfloat16 or wider, within the bound.
No kernel may reach another device: no remote copies, remote signals or barrier semaphores. Data moves between devices by JAX's collectives and lax.ppermute only.
A program may use at most 192 MiB of HBM per device.

```python
import math
import jax
import jax.numpy as jnp
from jax import lax

D = 2048
HEADS = 16
HEAD_WIDTH_SIZE = 128
BLOCK = 512
SEQ = 65536


def block_scale(own_key, shape, pieces, least, top_value):
    gain, own = 1.0, jax.random.fold_in(own_key, 6)
    for dim, blocks in pieces:
        draws = jnp.exp(jax.random.uniform(jax.random.fold_in(own, dim), (blocks,), jnp.float32, least / len(pieces), top_value / len(pieces)))
        gain = gain * jnp.repeat(draws, shape[dim] // blocks).reshape([-1 if axis == dim else 1 for axis in range(len(shape))])
    return gain


def noise(key, extent, scale, reach, pieces=(), held_as=jnp.bfloat16):
    array = jax.random.normal(key, extent, jnp.float32) * scale
    if len(pieces) > 0:
        array = block_scale(key, extent, pieces, -0.22, 0.18) * array
    return jnp.clip(array, min=-reach, max=reach).astype(held_as)


def setup_inputs(seed: int = 0) -> dict:
    splits = jax.random.split(jax.random.key(seed), 6)
    query_rows = noise(splits[0], (SEQ, D), 1.0, 6.0, ((0, 64), (1, 2)))
    key_rows = noise(splits[1], (SEQ, D), 1.0, 6.0, ((0, 64), (1, 2)))
    value_rows = noise(splits[2], (SEQ, D), 1.0, 6.0, ((0, 64), (1, 2)))
    out_grad = noise(splits[3], (SEQ, D), 1.0, 6.0, ((0, 64), (1, 2)))
    out_weight = noise(splits[4], (D, D), D ** -0.5, 0.125, ((0, 2),))
    return {"query_rows": query_rows, "key_rows": key_rows, "value_rows": value_rows, "out_grad": out_grad, "out_weight": out_weight}


def per_block_gradients(parts, scale_factor):
    qblock, kblock, vblock, gblock, key_running_state, gradient_tail_state = parts
    query_float = qblock.astype(jnp.float32)
    key_float = kblock.astype(jnp.float32)
    value_float = vblock.astype(jnp.float32)
    output_gradient_float = gblock.astype(jnp.float32)
    position = jnp.arange(BLOCK)
    causal = position[:, None] >= position[None, :]
    scores = jnp.einsum('thk,shk->hts', query_float, key_float)
    score_matrix = jnp.where(causal[None], scale_factor * scores, 0.0).astype(jnp.bfloat16).astype(jnp.float32)
    dscore = jnp.einsum('thv,shv->hts', output_gradient_float, value_float)
    weight_gradient = jnp.where(causal[None], scale_factor * dscore, 0.0).astype(jnp.bfloat16).astype(jnp.float32)
    maximal_precision_mode = lax.Precision.HIGHEST
    query_gradient = jnp.einsum('gye,ego->ygo', weight_gradient, key_float) + scale_factor * jnp.einsum('dic,inc->din', output_gradient_float, key_running_state, precision=maximal_precision_mode)
    key_gradient = jnp.einsum('uri,ruv->iuv', weight_gradient, query_float) + scale_factor * jnp.einsum('deg,epg->dep', value_float, gradient_tail_state, precision=maximal_precision_mode)
    value_gradient = jnp.einsum('rde,dru->eru', score_matrix, output_gradient_float) + scale_factor * jnp.einsum('leg,egu->leu', key_float, gradient_tail_state, precision=maximal_precision_mode)
    return (query_gradient.astype(jnp.bfloat16), key_gradient.astype(jnp.bfloat16), value_gradient.astype(jnp.bfloat16))

def reference(query_rows, key_rows, value_rows, out_grad, out_weight):
    scale_factor = 1.0 / math.sqrt(HEAD_WIDTH_SIZE * SEQ)
    head_grad = jnp.dot(out_grad, out_weight.T, preferred_element_type=jnp.float32).astype(jnp.bfloat16)
    blocks = SEQ // BLOCK
    shape_blocks = (blocks, BLOCK, HEADS, HEAD_WIDTH_SIZE)
    qblock = query_rows.reshape(shape_blocks)
    kblock = key_rows.reshape(shape_blocks)
    vblock = value_rows.reshape(shape_blocks)
    gblock = head_grad.reshape(shape_blocks)
    key_state = jnp.einsum('bthk,bthv->bhkv', kblock.astype(jnp.float32), vblock.astype(jnp.float32))
    grad_state = jnp.einsum('bthk,bthv->bhkv', qblock.astype(jnp.float32), gblock.astype(jnp.float32))
    key_running_state = jnp.cumsum(key_state, axis=0) - key_state
    gradient_tail_state = lax.optimization_barrier(jnp.sum(grad_state, axis=0))[None] - jnp.cumsum(grad_state, axis=0)
    query_gradient, key_gradient, value_gradient = lax.map(lambda parts: per_block_gradients(parts, scale_factor), (qblock, kblock, vblock, gblock, key_running_state, gradient_tail_state))
    return (query_gradient.reshape(SEQ, D), key_gradient.reshape(SEQ, D), value_gradient.reshape(SEQ, D))
```

```python
import functools
import math

import jax
import jax.numpy as jnp
from jax import lax
from jax.experimental import pallas as pl
from jax.experimental.pallas import tpu as pltpu
from jax.sharding import PartitionSpec as P

HEAD = 128
PAIR = 2 * HEAD
BLOCK = 512
F32, BF16 = jnp.float32, jnp.bfloat16
VMEM_LIMIT = 56 * 1024 * 1024


def dot(a, b, contract):
    return lax.dot_general(a, b, (((contract[0],), (contract[1],)), ((), ())), preferred_element_type=F32)


def pair_states(left, right):
    both = dot(left, right, (0, 0))
    return both[:HEAD, :HEAD], both[HEAD:, HEAD:]


def as_rows(state, rows):
    return state.astype(BF16).reshape(HEAD // rows, rows, HEAD)


def first_kernel(mine_ref, grad_ref, weight_ref, key_ref, value_ref, part_ref, state_ref):
    del mine_ref
    rows = state_ref.shape[1]
    part_ref[...] = dot(grad_ref[...], weight_ref[...], (1, 1))
    one, two = pair_states(key_ref[...], value_ref[...])
    state_ref[: HEAD // rows] = as_rows(one, rows)
    state_ref[HEAD // rows :] = as_rows(two, rows)


def second_kernel(mine_ref, grad_ref, weight_ref, part_ref, query_ref, state_ref, head_ref, sent_ref):
    del mine_ref
    rows = state_ref.shape[1]
    head_grad = (part_ref[...] + dot(grad_ref[...], weight_ref[...], (1, 1))).astype(BF16)
    head_ref[...] = head_grad
    one, two = pair_states(query_ref[...], head_grad)
    sent_ref[:, 0] = state_ref[...]
    sent_ref[: HEAD // rows, 1] = as_rows(one, rows)
    sent_ref[HEAD // rows :, 1] = as_rows(two, rows)


def inner_kernel(factor, query_ref, key_ref, value_ref, head_ref, dq_ref, dk_ref, dv_ref):
    length = query_ref.shape[0]
    blocks = length // BLOCK
    later = lax.broadcasted_iota(jnp.int32, (BLOCK, BLOCK), 0)
    earlier = lax.broadcasted_iota(jnp.int32, (BLOCK, BLOCK), 1)
    causal = earlier <= later
    keys = jnp.zeros((HEAD, HEAD), F32)
    for b in range(blocks):
        at = pl.ds(b * BLOCK, BLOCK)
        q, k, v, g = query_ref[at, :], key_ref[at, :], value_ref[at, :], head_ref[at, :]
        probs = jnp.where(causal, factor * dot(q, k, (1, 1)), 0.0).astype(BF16)
        weight = jnp.where(causal, factor * dot(g, v, (1, 1)), 0.0).astype(BF16)
        dq = dot(weight, k, (1, 0))
        if b > 0:
            dq = dq + dot(g, (factor * keys).astype(BF16), (1, 1))
        dq_ref[at, :] = dq.astype(dq_ref.dtype)
        dk_ref[at, :] = dot(weight, q, (0, 0)).astype(dk_ref.dtype)
        dv_ref[at, :] = dot(probs, g, (0, 0)).astype(dv_ref.dtype)
        if b < blocks - 1:
            keys = keys + dot(k, v, (0, 0))
    grads = jnp.zeros((HEAD, HEAD), F32)
    for b in reversed(range(blocks - 1)):
        after, at = pl.ds((b + 1) * BLOCK, BLOCK), pl.ds(b * BLOCK, BLOCK)
        grads = grads + dot(query_ref[after, :], head_ref[after, :], (0, 0))
        low = (factor * grads).astype(BF16)
        dk_ref[at, :] = (dk_ref[at, :] + dot(value_ref[at, :], low, (1, 1))).astype(dk_ref.dtype)
        dv_ref[at, :] = (dv_ref[at, :] + dot(key_ref[at, :], low, (1, 0))).astype(dv_ref.dtype)


def middle_kernel(factor, given_ref, carried_ref):
    count, _, rows, width = given_ref.shape
    total = jnp.zeros((rows, width), F32)
    for i in range(count):
        carried_ref[i, 0] = (factor * total).astype(BF16)
        total = total + given_ref[i, 0].astype(F32)
    total = jnp.zeros((rows, width), F32)
    for i in reversed(range(count)):
        carried_ref[i, 1] = (factor * total).astype(BF16)
        total = total + given_ref[i, 1].astype(F32)


def last_kernel(carried_ref, key_ref, value_ref, head_ref, dq_in, dk_in, dv_in, dq_ref, dk_ref, dv_ref):
    chunks = carried_ref.shape[0] // 2
    for h in range(2):
        here, cols = pl.ds(h * chunks, chunks), pl.ds(h * HEAD, HEAD)
        before = carried_ref[here, 0].reshape(HEAD, HEAD)
        after = carried_ref[here, 1].reshape(HEAD, HEAD)
        dq_ref[:, cols] = (dq_in[:, cols] + dot(head_ref[:, cols], before, (1, 1))).astype(BF16)
        dk_ref[:, cols] = (dk_in[:, cols] + dot(value_ref[:, cols], after, (1, 1))).astype(BF16)
        dv_ref[:, cols] = (dv_in[:, cols] + dot(key_ref[:, cols], after, (1, 0))).astype(BF16)


def per_device(query_rows, key_rows, value_rows, out_grad, out_weight):
    length, width = query_rows.shape
    count = lax.axis_size("ctx")
    pairs = width // PAIR
    factor = 1.0 / math.sqrt(HEAD * length * count)
    rows = width // count
    chunks = PAIR // rows
    params = pltpu.CompilerParams(vmem_limit_bytes=VMEM_LIMIT)

    other_grad = lax.ppermute(out_grad, "head", [(0, 1), (1, 0)])
    mine = lax.axis_index("head").astype(jnp.int32).reshape(1)

    whole = pl.BlockSpec((length, width), lambda j, m: (0, 0))
    column = pl.BlockSpec((length, PAIR), lambda j, m: (0, j))
    state = pl.BlockSpec((chunks, rows, HEAD), lambda j, m: (j, 0, 0))
    both = pl.BlockSpec((chunks, 2, rows, HEAD), lambda j, m: (j, 0, 0, 0))
    product = 2 * length * width * width
    part, key_state = pl.pallas_call(
        first_kernel,
        grid_spec=pltpu.PrefetchScalarGridSpec(
            num_scalar_prefetch=1,
            grid=(pairs,),
            in_specs=[whole, pl.BlockSpec((PAIR, width), lambda j, m: (j, m[0])), column, column],
            out_specs=[column, state],
        ),
        out_shape=[
            jax.ShapeDtypeStruct((length, width), F32),
            jax.ShapeDtypeStruct((count, rows, HEAD), BF16),
        ],
        compiler_params=params,
        cost_estimate=pl.CostEstimate(flops=product * 2, bytes_accessed=12 * length * width, transcendentals=0),
        name="own_part",
    )(mine, out_grad, out_weight, key_rows, value_rows)
    head_grad, sent = pl.pallas_call(
        second_kernel,
        grid_spec=pltpu.PrefetchScalarGridSpec(
            num_scalar_prefetch=1,
            grid=(pairs,),
            in_specs=[
                whole,
                pl.BlockSpec((PAIR, width), lambda j, m: (j, 1 - m[0])),
                column,
                column,
                state,
            ],
            out_specs=[column, both],
        ),
        out_shape=[
            jax.ShapeDtypeStruct((length, width), BF16),
            jax.ShapeDtypeStruct((count, 2, rows, HEAD), BF16),
        ],
        compiler_params=params,
        cost_estimate=pl.CostEstimate(flops=product * 2, bytes_accessed=12 * length * width, transcendentals=0),
        name="other_part",
    )(mine, other_grad, out_weight, part, query_rows, key_state)

    given = lax.all_to_all(sent, "ctx", 0, 0)

    head = pl.BlockSpec((length, HEAD), lambda h: (0, h))
    local = pl.pallas_call(
        functools.partial(inner_kernel, factor),
        grid=(width // HEAD,),
        in_specs=[head] * 4,
        out_specs=[head] * 3,
        out_shape=[jax.ShapeDtypeStruct((length, width), F32)] * 3,
        compiler_params=params,
        cost_estimate=pl.CostEstimate(flops=product * 4, bytes_accessed=20 * length * width, transcendentals=0),
        name="inner",
    )(query_rows, key_rows, value_rows, head_grad)

    carried = pl.pallas_call(
        functools.partial(middle_kernel, factor),
        out_shape=jax.ShapeDtypeStruct(given.shape, BF16),
        name="sums",
    )(given)
    carried = lax.all_to_all(carried, "ctx", 0, 0)

    column = pl.BlockSpec((length, PAIR), lambda j: (0, j))
    return pl.pallas_call(
        last_kernel,
        grid=(pairs,),
        in_specs=[pl.BlockSpec((chunks, 2, rows, HEAD), lambda j: (j, 0, 0, 0))] + [column] * 6,
        out_specs=[column] * 3,
        out_shape=[jax.ShapeDtypeStruct((length, width), BF16)] * 3,
        compiler_params=params,
        cost_estimate=pl.CostEstimate(flops=product, bytes_accessed=24 * length * width, transcendentals=0),
        name="carried_part",
    )(carried, key_rows, value_rows, head_grad, *local)


def solution(mesh):
    rows = P("ctx", "head")
    return jax.shard_map(
        per_device,
        mesh=mesh,
        in_specs=(rows, rows, rows, rows, P("head", None)),
        out_specs=(rows, rows, rows),
        check_vma=False,
    )
```

```python
import functools
import math

import jax
import jax.numpy as jnp
from jax import lax
from jax.experimental import pallas as pl
from jax.experimental.pallas import tpu as pltpu
from jax.sharding import PartitionSpec as P

HEAD = 128
PAIR = 2 * HEAD
BLOCK = 512
TILE = 256
F32, BF16 = jnp.float32, jnp.bfloat16
MIB = 1024 * 1024
IN_VMEM = pl.BlockSpec(memory_space=pltpu.VMEM)
ANYWHERE = pl.BlockSpec(memory_space=pl.ANY)


def near(*arrays):
    return [pltpu.with_memory_space_constraint(a, pltpu.VMEM) for a in arrays]


def far(*arrays):
    return [pltpu.with_memory_space_constraint(a, pltpu.HBM) for a in arrays]


def dot(a, b, contract):
    return lax.dot_general(a, b, (((contract[0],), (contract[1],)), ((), ())), preferred_element_type=F32)


def columns(j, size):
    return pl.ds(pl.multiple_of(j * size, size), size)


def of_head(h):
    return slice(h * HEAD, (h + 1) * HEAD)


def pair_states(left, right):
    both = dot(left, right, (0, 0))
    return both[:HEAD, :HEAD], both[HEAD:, HEAD:]


def as_rows(state, rows):
    return state.astype(BF16).reshape(HEAD // rows, rows, HEAD)


def first_kernel(mine_ref, grad_ref, weight_ref, key_ref, value_ref, part_ref, state_ref):
    del mine_ref
    rows = state_ref.shape[1]
    one, two = pair_states(key_ref[...], value_ref[...])
    state_ref[: HEAD // rows] = as_rows(one, rows)
    state_ref[HEAD // rows :] = as_rows(two, rows)
    part_ref[:, columns(pl.program_id(0), PAIR)] = dot(grad_ref[...], weight_ref[...], (1, 1))


def second_kernel(mine_ref, grad_ref, weight_ref, part_ref, query_ref, state_ref, head_ref, sent_ref, sum_ref):
    i = pl.program_id(0)
    width = grad_ref.shape[1]
    here = columns(i, TILE)
    other = dot(grad_ref[...], weight_ref[:, columns(1 - mine_ref[0], width)], (1, 1))
    head_ref[...] = (part_ref[here, :] + other).astype(BF16)

    @pl.when(i == 0)
    def _():
        sum_ref[...] = jnp.zeros_like(sum_ref)

    for h in range(width // HEAD):
        sum_ref[of_head(h), :] += dot(query_ref[here, of_head(h)], head_ref[:, of_head(h)], (0, 0))

    @pl.when(i == pl.num_programs(0) - 1)
    def _():
        sent_ref[:, 0] = state_ref[...]
        sent_ref[:, 1] = sum_ref[...].astype(BF16).reshape(state_ref.shape)


def inner_kernel(factor, after_ref, query_ref, key_ref, value_ref, head_ref, dq_ref, dk_ref, dv_ref):
    del after_ref
    blocks = query_ref.shape[0] // BLOCK
    later = lax.broadcasted_iota(jnp.int32, (BLOCK, BLOCK), 0)
    earlier = lax.broadcasted_iota(jnp.int32, (BLOCK, BLOCK), 1)
    causal = earlier <= later
    spans = [pl.ds(b * BLOCK, BLOCK) for b in range(blocks)]
    before, after = [None] * blocks, [None] * blocks
    for b in range(1, blocks):
        state = dot(key_ref[spans[b - 1], :], value_ref[spans[b - 1], :], (0, 0))
        before[b] = state if b == 1 else before[b - 1] + state
    for b in reversed(range(blocks - 1)):
        state = dot(query_ref[spans[b + 1], :], head_ref[spans[b + 1], :], (0, 0))
        after[b] = state if b == blocks - 2 else after[b + 1] + state
    for b, at in enumerate(spans):
        q, k, v, g = query_ref[at, :], key_ref[at, :], value_ref[at, :], head_ref[at, :]
        probs = jnp.where(causal, factor * dot(q, k, (1, 1)), 0.0).astype(BF16)
        weight = jnp.where(causal, factor * dot(g, v, (1, 1)), 0.0).astype(BF16)
        dq, dk, dv = dot(weight, k, (1, 0)), dot(weight, q, (0, 0)), dot(probs, g, (0, 0))
        if before[b] is not None:
            dq = dq + dot(g, (factor * before[b]).astype(BF16), (1, 1))
        if after[b] is not None:
            low = (factor * after[b]).astype(BF16)
            dk = dk + dot(v, low, (1, 1))
            dv = dv + dot(k, low, (1, 0))
        dq_ref[at, :], dk_ref[at, :], dv_ref[at, :] = dq.astype(BF16), dk.astype(BF16), dv.astype(BF16)


def middle_kernel(factor, given_ref, after_ref, carried_ref):
    del after_ref
    count, _, rows, width = given_ref.shape
    total = jnp.zeros((rows, width), F32)
    for i in range(count):
        carried_ref[i, 0] = (factor * total).astype(BF16)
        total = total + given_ref[i, 0].astype(F32)
    total = jnp.zeros((rows, width), F32)
    for i in reversed(range(count)):
        carried_ref[i, 1] = (factor * total).astype(BF16)
        total = total + given_ref[i, 1].astype(F32)


def last_kernel(carried_ref, key_ref, value_ref, head_ref, *refs):
    halves, (dq_ref, dk_ref, dv_ref) = (refs[:3], refs[3:6]), refs[6:]
    each = HEAD // carried_ref.shape[2]
    heads = key_ref.shape[1] // HEAD
    for h in range(heads):
        dq_in, dk_in, dv_in = halves[2 * h // heads]
        col, at = of_head(h), slice(h * each, (h + 1) * each)
        low = of_head(h % (heads // 2))
        before = carried_ref[at, 0].reshape(HEAD, HEAD)
        after = carried_ref[at, 1].reshape(HEAD, HEAD)
        dq_ref[:, col] = (dq_in[:, low] + dot(head_ref[:, col], before, (1, 1))).astype(BF16)
        dk_ref[:, col] = (dk_in[:, low] + dot(value_ref[:, col], after, (1, 1))).astype(BF16)
        dv_ref[:, col] = (dv_in[:, low] + dot(key_ref[:, col], after, (1, 0))).astype(BF16)


def per_device(query_rows, key_rows, value_rows, out_grad, out_weight):
    length, width = query_rows.shape
    count = lax.axis_size("ctx")
    pairs, heads = width // PAIR, width // HEAD
    factor = 1.0 / math.sqrt(HEAD * length * count)
    rows = width // count
    params = pltpu.CompilerParams(vmem_limit_bytes=16 * MIB)
    product = 2 * length * width * width
    area = length * width

    def cost(flops, bytes_accessed):
        return pl.CostEstimate(flops=int(flops), bytes_accessed=int(bytes_accessed), transcendentals=0)

    other_grad = lax.ppermute(out_grad, "head", [(0, 1), (1, 0)])
    mine = lax.axis_index("head").astype(jnp.int32).reshape(1)

    column = pl.BlockSpec((length, PAIR), lambda j, m: (0, j))
    part, key_state = pl.pallas_call(
        first_kernel,
        grid_spec=pltpu.PrefetchScalarGridSpec(
            num_scalar_prefetch=1,
            grid=(pairs,),
            in_specs=[
                pl.BlockSpec((length, width), lambda j, m: (0, 0)),
                pl.BlockSpec((PAIR, width), lambda j, m: (j, m[0])),
                column,
                column,
            ],
            out_specs=[IN_VMEM, pl.BlockSpec((PAIR // rows, rows, HEAD), lambda j, m: (j, 0, 0))],
        ),
        out_shape=[pltpu.VMEM((length, width), F32), jax.ShapeDtypeStruct((count, rows, HEAD), BF16)],
        compiler_params=params,
        cost_estimate=cost(2 * product, 8 * area),
        name="own_part",
    )(mine, *far(out_grad, out_weight, key_rows, value_rows))

    tile = pl.BlockSpec((TILE, width), lambda i, m: (i, 0))
    head_grad, sent = pl.pallas_call(
        second_kernel,
        grid_spec=pltpu.PrefetchScalarGridSpec(
            num_scalar_prefetch=1,
            grid=(length // TILE,),
            in_specs=[tile, IN_VMEM, IN_VMEM, IN_VMEM, IN_VMEM],
            out_specs=[tile, IN_VMEM],
            scratch_shapes=[pltpu.VMEM((width, HEAD), F32)],
        ),
        out_shape=[pltpu.HBM((length, width), BF16), pltpu.VMEM((count, 2, rows, HEAD), BF16)],
        compiler_params=params,
        cost_estimate=cost(2 * product, 8 * area),
        name="other_part",
    )(mine, *far(other_grad), *near(out_weight, part, query_rows, key_state))

    given = lax.all_to_all(sent, "ctx", 0, 0)

    def inner(base, number, after):
        return pl.pallas_call(
            functools.partial(inner_kernel, factor),
            grid=(number,),
            in_specs=[ANYWHERE] + [pl.BlockSpec((length, HEAD), lambda h: (0, h + base))] * 4,
            out_specs=[pl.BlockSpec((length, HEAD), lambda h: (0, h))] * 3,
            out_shape=[pltpu.HBM((length, number * HEAD), BF16)] * 3,
            compiler_params=params,
            cost_estimate=cost(6 * product * number / heads, 10 * area),
            name=f"inner_{base}",
        )(after, *far(query_rows, key_rows, value_rows, head_grad))

    half = heads // 2
    local_a = inner(0, half, key_state)
    carried = pl.pallas_call(
        functools.partial(middle_kernel, factor),
        in_specs=[IN_VMEM, ANYWHERE],
        out_specs=IN_VMEM,
        out_shape=pltpu.VMEM(given.shape, BF16),
        compiler_params=pltpu.CompilerParams(vmem_limit_bytes=4 * MIB),
        name="sums",
    )(*near(given), *far(local_a[0]))
    local_b = inner(half, heads - half, carried)
    carried = lax.all_to_all(carried, "ctx", 0, 0)

    tile = pl.BlockSpec((TILE, width), lambda i: (i, 0))
    return pl.pallas_call(
        last_kernel,
        grid=(length // TILE,),
        in_specs=[IN_VMEM] + [tile] * 3 + [pl.BlockSpec((TILE, width // 2), lambda i: (i, 0))] * 6,
        out_specs=[tile] * 3,
        out_shape=[jax.ShapeDtypeStruct((length, width), BF16)] * 3,
        compiler_params=params,
        cost_estimate=cost(product, 18 * area),
        name="carried_part",
    )(*near(carried), *far(key_rows, value_rows, head_grad, *local_a, *local_b))


def solution(mesh):
    rows = P("ctx", "head")
    return jax.shard_map(
        per_device,
        mesh=mesh,
        in_specs=(rows, rows, rows, rows, P("head", None)),
        out_specs=(rows, rows, rows),
        check_vma=False,
    )
```

```python
import functools
import math

import jax
import jax.numpy as jnp
from jax import lax
from jax.experimental import pallas as pl
from jax.experimental.pallas import tpu as pltpu
from jax.sharding import PartitionSpec as P

HEAD = 128
BLOCK = 512
TILE = 256
F32, BF16 = jnp.float32, jnp.bfloat16
MIB = 1024 * 1024
IN_VMEM = pl.BlockSpec(memory_space=pltpu.VMEM)
ANYWHERE = pl.BlockSpec(memory_space=pl.ANY)


def near(*arrays):
    return [pltpu.with_memory_space_constraint(a, pltpu.VMEM) for a in arrays]


def far(*arrays):
    return [pltpu.with_memory_space_constraint(a, pltpu.HBM) for a in arrays]


def dot(a, b, contract):
    return lax.dot_general(a, b, (((contract[0],), (contract[1],)), ((), ())), preferred_element_type=F32)


def columns(j, size):
    return pl.ds(pl.multiple_of(j * size, size), size)


def spans(length):
    return [pl.ds(i * TILE, TILE) for i in range(length // TILE)]


def put_states(left, right, write):
    for h in range(0, left.shape[1] // HEAD, 2):
        both = slice(h * HEAD, (h + 2) * HEAD)
        product = dot(left[:, both], right[:, both], (0, 0)).astype(BF16)
        write(h, product[:HEAD, :HEAD])
        write(h + 1, product[HEAD:, HEAD:])


def first_kernel(mine_ref, grad_hbm, weight_hbm, key_hbm, value_hbm, query_hbm, part_ref, state_ref, there_ref, query_ref,
                 grad_ref, here_ref, key_ref, value_ref, tile_sem, rest_sem):
    length, width = part_ref.shape
    rows = state_ref.shape[1]
    each = HEAD // rows
    tiles = spans(length)
    mine = mine_ref[0]
    grads, weights, keys, values = [
        [pltpu.make_async_copy(source.at[t, cols], target.at[t, :], tile_sem.at[n, i]) for i, t in enumerate(tiles)]
        for n, (source, target, cols) in enumerate(
            (
                (grad_hbm, grad_ref, slice(None)),
                (weight_hbm, here_ref, columns(mine, width)),
                (key_hbm, key_ref, slice(None)),
                (value_hbm, value_ref, slice(None)),
            )
        )
    ]
    rest = [
        pltpu.make_async_copy(weight_hbm.at[:, columns(1 - mine, width)], there_ref, rest_sem.at[0]),
        pltpu.make_async_copy(query_hbm, query_ref, rest_sem.at[1]),
    ]
    for copy in [grads[0], *weights, *grads[1:], *keys, *values, *rest]:
        copy.start()
    for copy in weights:
        copy.wait()
    for copy, t in zip(grads, tiles):
        copy.wait()
        part_ref[t, :] = dot(grad_ref[t, :], here_ref[...], (1, 1))
    for copy in [*keys, *values]:
        copy.wait()

    def write(h, state):
        state_ref[h * each : (h + 1) * each] = state.reshape(each, rows, HEAD)

    put_states(key_ref, value_ref, write)
    for copy in rest:
        copy.wait()


def second_kernel(grad_ref, weight_ref, part_ref, query_ref, state_ref, head_hbm, sent_ref, head_ref, sem):
    rows = state_ref.shape[1]
    each = HEAD // rows
    copies = []
    for i, t in enumerate(spans(part_ref.shape[0])):
        head_ref[t, :] = (part_ref[t, :] + dot(grad_ref[t, :], weight_ref[...], (1, 1))).astype(BF16)
        copies.append(pltpu.make_async_copy(head_ref.at[t, :], head_hbm.at[t, :], sem.at[i]))
        copies[-1].start()
    sent_ref[:, 0] = state_ref[...]

    def write(h, state):
        sent_ref[h * each : (h + 1) * each, 1] = state.reshape(each, rows, HEAD)

    put_states(query_ref, head_ref, write)
    for copy in copies:
        copy.wait()


def inner_kernel(factor, after_ref, query_ref, key_ref, value_ref, head_ref, dq_ref, dk_ref, dv_ref):
    del after_ref
    blocks = query_ref.shape[0] // BLOCK
    later = lax.broadcasted_iota(jnp.int32, (BLOCK, BLOCK), 0)
    earlier = lax.broadcasted_iota(jnp.int32, (BLOCK, BLOCK), 1)
    causal = earlier <= later
    parts = [pl.ds(b * BLOCK, BLOCK) for b in range(blocks)]
    before, after = [None] * blocks, [None] * blocks
    for b in range(1, blocks):
        state = dot(key_ref[parts[b - 1], :], value_ref[parts[b - 1], :], (0, 0))
        before[b] = state if b == 1 else before[b - 1] + state
    for b in reversed(range(blocks - 1)):
        state = dot(query_ref[parts[b + 1], :], head_ref[parts[b + 1], :], (0, 0))
        after[b] = state if b == blocks - 2 else after[b + 1] + state
    for b, at in enumerate(parts):
        q, k, v, g = query_ref[at, :], key_ref[at, :], value_ref[at, :], head_ref[at, :]
        probs = jnp.where(causal, factor * dot(q, k, (1, 1)), 0.0).astype(BF16)
        weight = jnp.where(causal, factor * dot(g, v, (1, 1)), 0.0).astype(BF16)
        dq, dk, dv = dot(weight, k, (1, 0)), dot(weight, q, (0, 0)), dot(probs, g, (0, 0))
        if before[b] is not None:
            dq = dq + dot(g, (factor * before[b]).astype(BF16), (1, 1))
        if after[b] is not None:
            low = (factor * after[b]).astype(BF16)
            dk = dk + dot(v, low, (1, 1))
            dv = dv + dot(k, low, (1, 0))
        for ref, value in ((dq_ref, dq), (dk_ref, dk), (dv_ref, dv)):
            out = slice(None) if ref.shape[1] == HEAD else columns(pl.program_id(0), HEAD)
            ref[at, out] = value.astype(BF16)


def middle_kernel(factor, given_ref, after_ref, carried_ref):
    del after_ref
    count, _, rows, width = given_ref.shape
    total = jnp.zeros((rows, width), F32)
    for i in range(count):
        carried_ref[i, 0] = (factor * total).astype(BF16)
        total = total + given_ref[i, 0].astype(F32)
    total = jnp.zeros((rows, width), F32)
    for i in reversed(range(count)):
        carried_ref[i, 1] = (factor * total).astype(BF16)
        total = total + given_ref[i, 1].astype(F32)


def two_heads(carried_ref, h, which):
    each = HEAD // carried_ref.shape[2]
    one = carried_ref[h * each : (h + 1) * each, which].reshape(HEAD, HEAD)
    two = carried_ref[(h + 1) * each : (h + 2) * each, which].reshape(HEAD, HEAD)
    none = jnp.zeros_like(one)
    return jnp.concatenate([jnp.concatenate([one, none], 1), jnp.concatenate([none, two], 1)], 0)


def last_kernel(carried_ref, key_ref, value_ref, head_ref, *refs):
    (dq_a, dk_a, dv_a, dq_b, dk_b, dv_b), (dq_ref, dk_ref, dv_ref) = refs[:6], refs[6:]
    here = columns(pl.program_id(0), TILE)
    heads = key_ref.shape[1] // HEAD
    for h in range(0, heads, 2):
        col = slice(h * HEAD, (h + 2) * HEAD)
        if h < heads // 2:
            dq_in, dk_in, dv_in = dq_a[:, col], dk_a[:, col], dv_a[:, col]
        else:
            low = slice((h - heads // 2) * HEAD, (h + 2 - heads // 2) * HEAD)
            dq_in, dk_in, dv_in = dq_b[here, low], dk_b[here, low], dv_b[:, low]
        before, after = two_heads(carried_ref, h, 0), two_heads(carried_ref, h, 1)
        dq_ref[:, col] = (dq_in + dot(head_ref[:, col], before, (1, 1))).astype(BF16)
        dk_ref[:, col] = (dk_in + dot(value_ref[:, col], after, (1, 1))).astype(BF16)
        dv_ref[:, col] = (dv_in + dot(key_ref[:, col], after, (1, 0))).astype(BF16)


def per_device(query_rows, key_rows, value_rows, out_grad, out_weight):
    length, width = query_rows.shape
    count = lax.axis_size("ctx")
    heads = width // HEAD
    factor = 1.0 / math.sqrt(HEAD * length * count)
    rows = width // count
    params = pltpu.CompilerParams(vmem_limit_bytes=16 * MIB)
    product = 2 * length * width * width
    area = length * width

    def cost(flops, bytes_accessed):
        return pl.CostEstimate(flops=int(flops), bytes_accessed=int(bytes_accessed), transcendentals=0)

    other_grad = lax.ppermute(out_grad, "head", [(0, 1), (1, 0)])
    mine = lax.axis_index("head").astype(jnp.int32).reshape(1)

    semaphores = pltpu.SemaphoreType.DMA
    tiles = length // TILE
    part, key_state, there, query_near = pl.pallas_call(
        first_kernel,
        in_specs=[pl.BlockSpec(memory_space=pltpu.SMEM)] + [ANYWHERE] * 5,
        out_specs=[IN_VMEM] * 4,
        out_shape=[
            pltpu.VMEM((length, width), F32),
            jax.ShapeDtypeStruct((count, rows, HEAD), BF16),
            pltpu.VMEM((width, width), BF16),
            pltpu.VMEM((length, width), BF16),
        ],
        scratch_shapes=[pltpu.VMEM((length, width), BF16)] * 4 + [semaphores((4, tiles)), semaphores((2,))],
        compiler_params=params,
        cost_estimate=cost(2 * product, 12 * area),
        name="own_part",
    )(mine, *far(out_grad, out_weight, key_rows, value_rows, query_rows))

    head_grad, sent = pl.pallas_call(
        second_kernel,
        in_specs=[IN_VMEM] * 5,
        out_specs=[ANYWHERE, IN_VMEM],
        out_shape=[pltpu.HBM((length, width), BF16), pltpu.VMEM((count, 2, rows, HEAD), BF16)],
        scratch_shapes=[pltpu.VMEM((length, width), BF16), semaphores((tiles,))],
        compiler_params=params,
        cost_estimate=cost(2 * product, 8 * area),
        name="other_part",
    )(*near(other_grad, there, part, query_near, key_state))

    given = lax.all_to_all(sent, "ctx", 0, 0)

    def inner(base, number, after, places):
        return pl.pallas_call(
            functools.partial(inner_kernel, factor),
            grid=(number,),
            in_specs=[ANYWHERE] + [pl.BlockSpec((length, HEAD), lambda h: (0, h + base))] * 4,
            out_specs=[IN_VMEM if p is pltpu.VMEM else pl.BlockSpec((length, HEAD), lambda h: (0, h)) for p in places],
            out_shape=[p((length, number * HEAD), BF16) for p in places],
            compiler_params=params,
            cost_estimate=cost(6 * product * number / heads, 10 * area),
            name=f"inner_{base}",
        )(after, *far(query_rows, key_rows, value_rows, head_grad))

    half = heads // 2
    local_a = inner(0, half, key_state, [pltpu.HBM] * 3)
    carried = pl.pallas_call(
        functools.partial(middle_kernel, factor),
        in_specs=[IN_VMEM, ANYWHERE],
        out_specs=IN_VMEM,
        out_shape=pltpu.VMEM(given.shape, BF16),
        compiler_params=pltpu.CompilerParams(vmem_limit_bytes=4 * MIB),
        name="sums",
    )(*near(given), *far(local_a[0]))
    local_b = inner(half, heads - half, carried, [pltpu.VMEM, pltpu.VMEM, pltpu.HBM])
    carried = lax.all_to_all(carried, "ctx", 0, 0)

    tile = pl.BlockSpec((TILE, width), lambda i: (i, 0))
    half_tile = pl.BlockSpec((TILE, width // 2), lambda i: (i, 0))
    return pl.pallas_call(
        last_kernel,
        grid=(length // TILE,),
        in_specs=[IN_VMEM] + [tile] * 3 + [half_tile] * 3 + [IN_VMEM, IN_VMEM, half_tile],
        out_specs=[tile] * 3,
        out_shape=[jax.ShapeDtypeStruct((length, width), BF16)] * 3,
        compiler_params=params,
        cost_estimate=cost(product, 18 * area),
        name="carried_part",
    )(*near(carried), *far(key_rows, value_rows, head_grad, *local_a), *near(*local_b[:2]), *far(local_b[2]))


def solution(mesh):
    rows = P("ctx", "head")
    return jax.shard_map(
        per_device,
        mesh=mesh,
        in_specs=(rows, rows, rows, rows, P("head", None)),
        out_specs=(rows, rows, rows),
        check_vma=False,
    )
```

```python
import functools
import math

import jax
import jax.numpy as jnp
from jax import lax
from jax.experimental import pallas as pl
from jax.experimental.pallas import tpu as pltpu
from jax.sharding import PartitionSpec as P

HEAD = 128
BLOCK = 256
PAIR = 2 * HEAD
TILE = 256
F32, BF16 = jnp.float32, jnp.bfloat16
MIB = 1024 * 1024
IN_VMEM = pl.BlockSpec(memory_space=pltpu.VMEM)
ANYWHERE = pl.BlockSpec(memory_space=pl.ANY)


def near(*arrays):
    return [pltpu.with_memory_space_constraint(a, pltpu.VMEM) for a in arrays]


def far(*arrays):
    return [pltpu.with_memory_space_constraint(a, pltpu.HBM) for a in arrays]


def dot(a, b, contract):
    return lax.dot_general(a, b, (((contract[0],), (contract[1],)), ((), ())), preferred_element_type=F32)


def columns(j, size):
    return pl.ds(pl.multiple_of(j * size, size), size)


def spans(length):
    return [pl.ds(i * TILE, TILE) for i in range(length // TILE)]


def put_states(left, right, write):
    for h in range(0, left.shape[1] // HEAD, 2):
        both = slice(h * HEAD, (h + 2) * HEAD)
        product = dot(left[:, both], right[:, both], (0, 0)).astype(BF16)
        write(h, product[:HEAD, :HEAD])
        write(h + 1, product[HEAD:, HEAD:])


def first_kernel(mine_ref, grad_hbm, weight_hbm, key_hbm, value_hbm, part_ref, state_ref, there_ref,
                 grad_ref, here_ref, key_ref, value_ref, tile_sem, rest_sem):
    length, width = part_ref.shape
    rows = state_ref.shape[1]
    each = HEAD // rows
    tiles = spans(length)
    mine = mine_ref[0]
    grads, weights, keys, values = [
        [pltpu.make_async_copy(source.at[t, cols], target.at[t, :], tile_sem.at[n, i]) for i, t in enumerate(tiles)]
        for n, (source, target, cols) in enumerate(
            (
                (grad_hbm, grad_ref, slice(None)),
                (weight_hbm, here_ref, columns(mine, width)),
                (key_hbm, key_ref, slice(None)),
                (value_hbm, value_ref, slice(None)),
            )
        )
    ]
    rest = pltpu.make_async_copy(weight_hbm.at[:, columns(1 - mine, width)], there_ref, rest_sem)
    for copy in [grads[0], *weights, *grads[1:], *keys, *values, rest]:
        copy.start()
    for copy in weights:
        copy.wait()
    for copy, t in zip(grads, tiles):
        copy.wait()
        part_ref[t, :] = dot(grad_ref[t, :], here_ref[...], (1, 1))
    for copy in [*keys, *values]:
        copy.wait()

    def write(h, state):
        state_ref[h * each : (h + 1) * each] = state.reshape(each, rows, HEAD)

    put_states(key_ref, value_ref, write)
    rest.wait()


def second_kernel(grad_ref, weight_ref, part_ref, query_hbm, state_ref, head_hbm, sent_ref, query_ref, head_ref, sem, query_sem):
    rows = state_ref.shape[1]
    each = HEAD // rows
    fetch = pltpu.make_async_copy(query_hbm, query_ref, query_sem)
    fetch.start()
    copies = []
    for i, t in enumerate(spans(part_ref.shape[0])):
        head_ref[t, :] = (part_ref[t, :] + dot(grad_ref[t, :], weight_ref[...], (1, 1))).astype(BF16)
        copies.append(pltpu.make_async_copy(head_ref.at[t, :], head_hbm.at[t, :], sem.at[i]))
        copies[-1].start()
    sent_ref[:, 0] = state_ref[...]

    def write(h, state):
        sent_ref[h * each : (h + 1) * each, 1] = state.reshape(each, rows, HEAD)

    fetch.wait()
    put_states(query_ref, head_ref, write)
    for copy in copies:
        copy.wait()


def inner_kernel(factor, after_ref, query_ref, key_ref, value_ref, head_ref, dq_ref, dk_ref, dv_ref):
    del after_ref
    blocks = query_ref.shape[0] // BLOCK
    down = lax.broadcasted_iota(jnp.int32, (BLOCK, BLOCK), 0)
    across = lax.broadcasted_iota(jnp.int32, (BLOCK, BLOCK), 1)
    left_head = lax.broadcasted_iota(jnp.int32, (PAIR, PAIR), 0) < HEAD
    same_head = left_head == (lax.broadcasted_iota(jnp.int32, (PAIR, PAIR), 1) < HEAD)
    parts = [pl.ds(b * BLOCK, BLOCK) for b in range(blocks)]

    def lowered(state):
        return jnp.where(same_head, factor * state, 0.0).astype(BF16)

    def scores(keep, left, right):
        return jnp.where(keep, factor * dot(left, right, (1, 1)), 0.0).astype(BF16)

    before, after = [None] * blocks, [None] * blocks
    for b in range(1, blocks):
        state = dot(key_ref[parts[b - 1], :], value_ref[parts[b - 1], :], (0, 0))
        before[b] = state if b == 1 else before[b - 1] + state
    for b in reversed(range(blocks - 1)):
        state = dot(query_ref[parts[b + 1], :], head_ref[parts[b + 1], :], (0, 0))
        after[b] = state if b == blocks - 2 else after[b + 1] + state
    for b, at in enumerate(parts):
        sums = [None] * 3
        if before[b] is not None:
            sums[0] = dot(head_ref[at, :], lowered(before[b]), (1, 1))
        if after[b] is not None:
            low = lowered(after[b])
            sums[1:] = dot(value_ref[at, :], low, (1, 1)), dot(key_ref[at, :], low, (1, 0))
        for h in range(2):
            col = slice(h * HEAD, (h + 1) * HEAD)
            q, k, v, g = query_ref[at, col], key_ref[at, col], value_ref[at, col], head_ref[at, col]
            values = [
                dot(scores(across <= down, g, v), k, (1, 0)),
                dot(scores(down <= across, v, g), q, (1, 0)),
                dot(scores(down <= across, k, q), g, (1, 0)),
            ]
            for ref, value, extra in zip((dq_ref, dk_ref, dv_ref), values, sums):
                if extra is not None:
                    value = value + extra[:, col]
                out = col if ref.shape[1] == PAIR else columns(2 * pl.program_id(0) + h, HEAD)
                ref[at, out] = value.astype(BF16)


def middle_kernel(factor, given_ref, after_ref, carried_ref):
    del after_ref
    count, _, rows, width = given_ref.shape
    total = jnp.zeros((rows, width), F32)
    for i in range(count):
        carried_ref[i, 0] = (factor * total).astype(BF16)
        total = total + given_ref[i, 0].astype(F32)
    total = jnp.zeros((rows, width), F32)
    for i in reversed(range(count)):
        carried_ref[i, 1] = (factor * total).astype(BF16)
        total = total + given_ref[i, 1].astype(F32)


def two_heads(carried_ref, h, which):
    each = HEAD // carried_ref.shape[2]
    one = carried_ref[h * each : (h + 1) * each, which].reshape(HEAD, HEAD)
    two = carried_ref[(h + 1) * each : (h + 2) * each, which].reshape(HEAD, HEAD)
    none = jnp.zeros_like(one)
    return jnp.concatenate([jnp.concatenate([one, none], 1), jnp.concatenate([none, two], 1)], 0)


def last_kernel(carried_ref, key_hbm, value_hbm, head_hbm, dq_a, dk_a, dv_a, dq_b, dk_b, dv_b, dq_hbm, dk_hbm, dv_hbm, *refs):
    inputs, outputs, (sem, out_sem) = refs[:7], refs[7:10], refs[10:]
    sources, targets = (head_hbm, dq_a, value_hbm, dk_a, key_hbm, dv_a, dv_b), (dq_hbm, dk_hbm, dv_hbm)
    length, width = outputs[0].shape
    edges = [0, TILE // 2, *range(TILE // 2 + TILE, length, TILE), length]
    tiles = [pl.ds(a, b - a) for a, b in zip(edges, edges[1:])]
    loads = [
        [pltpu.make_async_copy(a.at[t, :], b.at[t, :], sem.at[n, i]) for n, (a, b) in enumerate(zip(sources, inputs))]
        for i, t in enumerate(tiles)
    ]
    stores = [
        [pltpu.make_async_copy(a.at[t, :], b.at[t, :], out_sem.at[n, i]) for n, (a, b) in enumerate(zip(outputs, targets))]
        for i, t in enumerate(tiles)
    ]
    for copy in sum(loads, []):
        copy.start()
    states = [(two_heads(carried_ref, h, 0), two_heads(carried_ref, h, 1)) for h in range(0, width // HEAD, 2)]
    half = width // 2
    grads, dq_in, values, dk_in, keys, dv_in, dv_rest = inputs
    for i, t in enumerate(tiles):
        for copy in loads[i]:
            copy.wait()
        for j, (before, after) in enumerate(states):
            col = slice(j * PAIR, (j + 1) * PAIR)
            if j * PAIR < half:
                locals_ = dq_in[t, col], dk_in[t, col], dv_in[t, col]
            else:
                low = slice(j * PAIR - half, (j + 1) * PAIR - half)
                locals_ = dq_b[t, low], dk_b[t, low], dv_rest[t, low]
            sums = dot(grads[t, col], before, (1, 1)), dot(values[t, col], after, (1, 1)), dot(keys[t, col], after, (1, 0))
            for ref, own, carried in zip(outputs, locals_, sums):
                ref[t, col] = (own + carried).astype(BF16)
        for copy in stores[i]:
            copy.start()
    for copy in sum(stores, []):
        copy.wait()


def per_device(query_rows, key_rows, value_rows, out_grad, out_weight):
    length, width = query_rows.shape
    count = lax.axis_size("ctx")
    heads = width // HEAD
    factor = 1.0 / math.sqrt(HEAD * length * count)
    rows = width // count
    params = pltpu.CompilerParams(vmem_limit_bytes=16 * MIB)
    product = 2 * length * width * width
    area = length * width

    def cost(flops, bytes_accessed):
        return pl.CostEstimate(flops=int(flops), bytes_accessed=int(bytes_accessed), transcendentals=0)

    other_grad = lax.ppermute(out_grad, "head", [(0, 1), (1, 0)])
    mine = lax.axis_index("head").astype(jnp.int32).reshape(1)

    semaphores = pltpu.SemaphoreType.DMA
    tiles = length // TILE
    part, key_state, there = pl.pallas_call(
        first_kernel,
        in_specs=[pl.BlockSpec(memory_space=pltpu.SMEM)] + [ANYWHERE] * 4,
        out_specs=[IN_VMEM] * 3,
        out_shape=[
            pltpu.VMEM((length, width), F32),
            jax.ShapeDtypeStruct((count, rows, HEAD), BF16),
            pltpu.VMEM((width, width), BF16),
        ],
        scratch_shapes=[pltpu.VMEM((length, width), BF16)] * 4 + [semaphores((4, tiles)), semaphores],
        compiler_params=params,
        cost_estimate=cost(2 * product, 12 * area),
        name="own_part",
    )(mine, *far(out_grad, out_weight, key_rows, value_rows))

    head_grad, sent = pl.pallas_call(
        second_kernel,
        in_specs=[IN_VMEM] * 3 + [ANYWHERE, IN_VMEM],
        out_specs=[ANYWHERE, IN_VMEM],
        out_shape=[pltpu.HBM((length, width), BF16), pltpu.VMEM((count, 2, rows, HEAD), BF16)],
        scratch_shapes=[pltpu.VMEM((length, width), BF16)] * 2 + [semaphores((tiles,)), semaphores],
        compiler_params=params,
        cost_estimate=cost(2 * product, 8 * area),
        name="other_part",
    )(*near(other_grad, there, part), *far(query_rows), *near(key_state))

    given = lax.all_to_all(sent, "ctx", 0, 0)

    def inner(base, number, after, places):
        return pl.pallas_call(
            functools.partial(inner_kernel, factor),
            grid=(number // 2,),
            in_specs=[ANYWHERE] + [pl.BlockSpec((length, PAIR), lambda h: (0, h + base // 2))] * 4,
            out_specs=[IN_VMEM if p is pltpu.VMEM else pl.BlockSpec((length, PAIR), lambda h: (0, h)) for p in places],
            out_shape=[p((length, number * HEAD), BF16) for p in places],
            compiler_params=params,
            cost_estimate=cost(6 * product * number / heads, 10 * area),
            name=f"inner_{base}",
        )(after, *far(query_rows, key_rows, value_rows, head_grad))

    half = heads // 2
    local_a = inner(0, half, key_state, [pltpu.HBM] * 3)
    carried = pl.pallas_call(
        functools.partial(middle_kernel, factor),
        in_specs=[IN_VMEM, ANYWHERE],
        out_specs=IN_VMEM,
        out_shape=pltpu.VMEM(given.shape, BF16),
        compiler_params=pltpu.CompilerParams(vmem_limit_bytes=4 * MIB),
        name="sums",
    )(*near(given), *far(local_a[0]))
    local_b = inner(half, heads - half, carried, [pltpu.VMEM, pltpu.VMEM, pltpu.HBM])
    carried = lax.all_to_all(carried, "ctx", 0, 0)

    full, part_width = pltpu.VMEM((length, width), BF16), pltpu.VMEM((length, width // 2), BF16)
    steps = tiles + 1
    return pl.pallas_call(
        last_kernel,
        in_specs=[IN_VMEM] + [ANYWHERE] * 6 + [IN_VMEM] * 2 + [ANYWHERE],
        out_specs=[ANYWHERE] * 3,
        out_shape=[jax.ShapeDtypeStruct((length, width), BF16)] * 3,
        scratch_shapes=[full, part_width, full, part_width, full, part_width, part_width, full, full, full]
        + [semaphores((7, steps)), semaphores((3, steps))],
        compiler_params=pltpu.CompilerParams(vmem_limit_bytes=24 * MIB),
        cost_estimate=cost(product, 18 * area),
        name="carried_part",
    )(*near(carried), *far(key_rows, value_rows, head_grad, *local_a), *near(*local_b[:2]), *far(local_b[2]))


def solution(mesh):
    rows = P("ctx", "head")
    return jax.shard_map(
        per_device,
        mesh=mesh,
        in_specs=(rows, rows, rows, rows, P("head", None)),
        out_specs=(rows, rows, rows),
        check_vma=False,
    )
```

```python
import functools
import math

import jax
import jax.numpy as jnp
from jax import lax
from jax.experimental import pallas as pl
from jax.experimental.pallas import tpu as pltpu
from jax.sharding import PartitionSpec as P

HEAD = 128
BLOCK = 256
PAIR = 2 * HEAD
TILE = 256
F32, BF16 = jnp.float32, jnp.bfloat16
MIB = 1024 * 1024
IN_VMEM = pl.BlockSpec(memory_space=pltpu.VMEM)
ANYWHERE = pl.BlockSpec(memory_space=pl.ANY)


def near(*arrays):
    return [pltpu.with_memory_space_constraint(a, pltpu.VMEM) for a in arrays]


def far(*arrays):
    return [pltpu.with_memory_space_constraint(a, pltpu.HBM) for a in arrays]


def dot(a, b, contract):
    return lax.dot_general(a, b, (((contract[0],), (contract[1],)), ((), ())), preferred_element_type=F32)


def columns(j, size):
    return pl.ds(pl.multiple_of(j * size, size), size)


def spans(length):
    return [pl.ds(i * TILE, TILE) for i in range(length // TILE)]


def put_states(left, right, write):
    for h in range(0, left.shape[1] // HEAD, 2):
        both = slice(h * HEAD, (h + 2) * HEAD)
        product = dot(left[:, both], right[:, both], (0, 0)).astype(BF16)
        write(h, product[:HEAD, :HEAD])
        write(h + 1, product[HEAD:, HEAD:])


def first_kernel(mine_ref, grad_hbm, weight_hbm, key_hbm, value_hbm, part_ref, state_ref, there_ref,
                 grad_ref, here_ref, key_ref, value_ref, tile_sem, rest_sem):
    length, width = part_ref.shape
    rows = state_ref.shape[1]
    each = HEAD // rows
    tiles = spans(length)
    mine = mine_ref[0]
    grads, weights, keys, values = [
        [pltpu.make_async_copy(source.at[t, cols], target.at[t, :], tile_sem.at[n, i]) for i, t in enumerate(tiles)]
        for n, (source, target, cols) in enumerate(
            (
                (grad_hbm, grad_ref, slice(None)),
                (weight_hbm, here_ref, columns(mine, width)),
                (key_hbm, key_ref, slice(None)),
                (value_hbm, value_ref, slice(None)),
            )
        )
    ]
    rest = pltpu.make_async_copy(weight_hbm.at[:, columns(1 - mine, width)], there_ref, rest_sem)
    for copy in [grads[0], *weights, *grads[1:], *keys, *values, rest]:
        copy.start()
    for copy in weights:
        copy.wait()
    for copy, t in zip(grads, tiles):
        copy.wait()
        part_ref[t, :] = dot(grad_ref[t, :], here_ref[...], (1, 1))
    for copy in [*keys, *values]:
        copy.wait()

    def write(h, state):
        state_ref[h * each : (h + 1) * each] = state.reshape(each, rows, HEAD)

    put_states(key_ref, value_ref, write)
    rest.wait()


def second_kernel(grad_ref, weight_ref, part_ref, query_hbm, state_ref, head_hbm, sent_ref, query_ref, head_ref, sem, query_sem):
    rows = state_ref.shape[1]
    each = HEAD // rows
    fetch = pltpu.make_async_copy(query_hbm, query_ref, query_sem)
    fetch.start()
    copies = []
    for i, t in enumerate(spans(part_ref.shape[0])):
        head_ref[t, :] = (part_ref[t, :] + dot(grad_ref[t, :], weight_ref[...], (1, 1))).astype(BF16)
        copies.append(pltpu.make_async_copy(head_ref.at[t, :], head_hbm.at[t, :], sem.at[i]))
        copies[-1].start()
    sent_ref[:, 0] = state_ref[...]

    def write(h, state):
        sent_ref[h * each : (h + 1) * each, 1] = state.reshape(each, rows, HEAD)

    fetch.wait()
    put_states(query_ref, head_ref, write)
    for copy in copies:
        copy.wait()


def inner_kernel(factor, after_ref, query_ref, key_ref, value_ref, head_ref, dq_ref, dk_ref, dv_ref, before_ref, behind_ref):
    del after_ref
    blocks = query_ref.shape[0] // BLOCK
    down = lax.broadcasted_iota(jnp.int32, (BLOCK, BLOCK), 0)
    across = lax.broadcasted_iota(jnp.int32, (BLOCK, BLOCK), 1)
    left_head = lax.broadcasted_iota(jnp.int32, (PAIR, PAIR), 0) < HEAD
    same_head = left_head == (lax.broadcasted_iota(jnp.int32, (PAIR, PAIR), 1) < HEAD)
    parts = [pl.ds(b * BLOCK, BLOCK) for b in range(blocks)]

    def lowered(state):
        return jnp.where(same_head, factor * state, 0.0).astype(BF16)

    def scores(keep, left, right):
        return jnp.where(keep, factor * dot(left, right, (1, 1)), 0.0).astype(BF16)

    state = None
    for b in range(1, blocks):
        step = dot(key_ref[parts[b - 1], :], value_ref[parts[b - 1], :], (0, 0))
        state = step if state is None else state + step
        before_ref[b] = lowered(state)
    state = None
    for b in reversed(range(blocks - 1)):
        step = dot(query_ref[parts[b + 1], :], head_ref[parts[b + 1], :], (0, 0))
        state = step if state is None else state + step
        behind_ref[b] = lowered(state)
    for b, at in enumerate(parts):
        sums = [None] * 3
        if b > 0:
            sums[0] = dot(head_ref[at, :], before_ref[b], (1, 1))
        if b < blocks - 1:
            low = behind_ref[b]
            sums[1:] = dot(value_ref[at, :], low, (1, 1)), dot(key_ref[at, :], low, (1, 0))
        for h in range(2):
            col = slice(h * HEAD, (h + 1) * HEAD)
            q, k, v, g = query_ref[at, col], key_ref[at, col], value_ref[at, col], head_ref[at, col]
            values = [
                dot(scores(across <= down, g, v), k, (1, 0)),
                dot(scores(down <= across, v, g), q, (1, 0)),
                dot(scores(down <= across, k, q), g, (1, 0)),
            ]
            for ref, value, extra in zip((dq_ref, dk_ref, dv_ref), values, sums):
                if extra is not None:
                    value = value + extra[:, col]
                out = col if ref.shape[1] == PAIR else columns(2 * pl.program_id(0) + h, HEAD)
                ref[at, out] = value.astype(BF16)


def middle_kernel(factor, given_ref, after_ref, carried_ref):
    del after_ref
    count, _, rows, width = given_ref.shape
    total = jnp.zeros((rows, width), F32)
    for i in reversed(range(count)):
        carried_ref[i, 0] = (factor * total).astype(BF16)
        total = total + given_ref[i, 0].astype(F32)
    total = jnp.zeros((rows, width), F32)
    for i in range(count):
        carried_ref[i, 1] = (factor * total).astype(BF16)
        total = total + given_ref[i, 1].astype(F32)


def two_heads(carried_ref, h, which):
    each = HEAD // carried_ref.shape[2]
    one = carried_ref[h * each : (h + 1) * each, which].reshape(HEAD, HEAD)
    two = carried_ref[(h + 1) * each : (h + 2) * each, which].reshape(HEAD, HEAD)
    none = jnp.zeros_like(one)
    return jnp.concatenate([jnp.concatenate([one, none], 1), jnp.concatenate([none, two], 1)], 0)


def last_kernel(carried_ref, key_hbm, value_hbm, head_hbm, dq_a, dk_a, dv_a, dq_b, dk_b, dv_b, dq_hbm, dk_hbm, dv_hbm, *refs):
    inputs, outputs, (sem, out_sem) = refs[:7], refs[7:10], refs[10:]
    sources, targets = (head_hbm, dq_a, value_hbm, dk_a, key_hbm, dv_a, dv_b), (dq_hbm, dk_hbm, dv_hbm)
    length, width = outputs[0].shape
    edges = [0, TILE // 2, *range(TILE // 2 + TILE, length, TILE), length]
    tiles = [pl.ds(a, b - a) for a, b in zip(edges, edges[1:])]
    loads = [
        [pltpu.make_async_copy(a.at[t, :], b.at[t, :], sem.at[n, i]) for n, (a, b) in enumerate(zip(sources, inputs))]
        for i, t in enumerate(tiles)
    ]
    stores = [
        [pltpu.make_async_copy(a.at[t, :], b.at[t, :], out_sem.at[n, i]) for n, (a, b) in enumerate(zip(outputs, targets))]
        for i, t in enumerate(tiles)
    ]
    for copy in sum(loads, []):
        copy.start()
    states = [(two_heads(carried_ref, h, 0), two_heads(carried_ref, h, 1)) for h in range(0, width // HEAD, 2)]
    half = width // 2
    grads, dq_in, values, dk_in, keys, dv_in, dv_rest = inputs
    for i, t in enumerate(tiles):
        for copy in loads[i]:
            copy.wait()
        for j, (before, after) in enumerate(states):
            col = slice(j * PAIR, (j + 1) * PAIR)
            if j * PAIR < half:
                locals_ = dq_in[t, col], dk_in[t, col], dv_in[t, col]
            else:
                low = slice(j * PAIR - half, (j + 1) * PAIR - half)
                locals_ = dq_b[t, low], dk_b[t, low], dv_rest[t, low]
            sums = dot(grads[t, col], before, (1, 1)), dot(values[t, col], after, (1, 1)), dot(keys[t, col], after, (1, 0))
            for ref, own, carried in zip(outputs, locals_, sums):
                ref[t, col] = (own + carried).astype(BF16)
        for copy in stores[i]:
            copy.start()
    for copy in sum(stores, []):
        copy.wait()


def per_device(query_rows, key_rows, value_rows, out_grad, out_weight):
    length, width = query_rows.shape
    count = lax.axis_size("ctx")
    order = [list(reversed(range(count)))]
    heads = width // HEAD
    factor = 1.0 / math.sqrt(HEAD * length * count)
    rows = width // count
    params = pltpu.CompilerParams(vmem_limit_bytes=16 * MIB)
    product = 2 * length * width * width
    area = length * width

    def cost(flops, bytes_accessed):
        return pl.CostEstimate(flops=int(flops), bytes_accessed=int(bytes_accessed), transcendentals=0)

    other_grad = lax.ppermute(out_grad, "head", [(0, 1), (1, 0)])
    mine = lax.axis_index("head").astype(jnp.int32).reshape(1)

    semaphores = pltpu.SemaphoreType.DMA
    tiles = length // TILE
    part, key_state, there = pl.pallas_call(
        first_kernel,
        in_specs=[pl.BlockSpec(memory_space=pltpu.SMEM)] + [ANYWHERE] * 4,
        out_specs=[IN_VMEM] * 3,
        out_shape=[
            pltpu.VMEM((length, width), F32),
            jax.ShapeDtypeStruct((count, rows, HEAD), BF16),
            pltpu.VMEM((width, width), BF16),
        ],
        scratch_shapes=[pltpu.VMEM((length, width), BF16)] * 4 + [semaphores((4, tiles)), semaphores],
        compiler_params=params,
        cost_estimate=cost(2 * product, 12 * area),
        name="own_part",
    )(mine, *far(out_grad, out_weight, key_rows, value_rows))

    head_grad, sent = pl.pallas_call(
        second_kernel,
        in_specs=[IN_VMEM] * 3 + [ANYWHERE, IN_VMEM],
        out_specs=[ANYWHERE, IN_VMEM],
        out_shape=[pltpu.HBM((length, width), BF16), pltpu.VMEM((count, 2, rows, HEAD), BF16)],
        scratch_shapes=[pltpu.VMEM((length, width), BF16)] * 2 + [semaphores((tiles,)), semaphores],
        compiler_params=params,
        cost_estimate=cost(2 * product, 8 * area),
        name="other_part",
    )(*near(other_grad, there, part), *far(query_rows), *near(key_state))

    given = lax.all_to_all(sent, "ctx", 0, 0, axis_index_groups=order)

    def inner(base, number, after, places):
        return pl.pallas_call(
            functools.partial(inner_kernel, factor),
            grid=(number // 2,),
            in_specs=[ANYWHERE] + [pl.BlockSpec((length, PAIR), lambda h: (0, h + base // 2))] * 4,
            out_specs=[IN_VMEM if p is pltpu.VMEM else pl.BlockSpec((length, PAIR), lambda h: (0, h)) for p in places],
            out_shape=[p((length, number * HEAD), BF16) for p in places],
            scratch_shapes=[pltpu.VMEM((length // BLOCK, PAIR, PAIR), BF16)] * 2,
            compiler_params=params,
            cost_estimate=cost(6 * product * number / heads, 10 * area),
            name=f"inner_{base}",
        )(after, *far(query_rows, key_rows, value_rows, head_grad))

    half = heads // 2
    local_a = inner(0, half, key_state, [pltpu.HBM] * 3)
    carried = pl.pallas_call(
        functools.partial(middle_kernel, factor),
        in_specs=[IN_VMEM, ANYWHERE],
        out_specs=IN_VMEM,
        out_shape=pltpu.VMEM(given.shape, BF16),
        compiler_params=pltpu.CompilerParams(vmem_limit_bytes=4 * MIB),
        name="sums",
    )(*near(given), *far(local_a[0]))
    local_b = inner(half, heads - half, carried, [pltpu.VMEM, pltpu.VMEM, pltpu.HBM])
    carried = lax.all_to_all(carried, "ctx", 0, 0, axis_index_groups=order)

    full, part_width = pltpu.VMEM((length, width), BF16), pltpu.VMEM((length, width // 2), BF16)
    steps = tiles + 1
    return pl.pallas_call(
        last_kernel,
        in_specs=[IN_VMEM] + [ANYWHERE] * 6 + [IN_VMEM] * 2 + [ANYWHERE],
        out_specs=[ANYWHERE] * 3,
        out_shape=[jax.ShapeDtypeStruct((length, width), BF16)] * 3,
        scratch_shapes=[full, part_width, full, part_width, full, part_width, part_width, full, full, full]
        + [semaphores((7, steps)), semaphores((3, steps))],
        compiler_params=pltpu.CompilerParams(vmem_limit_bytes=24 * MIB),
        cost_estimate=cost(product, 18 * area),
        name="carried_part",
    )(*near(carried), *far(key_rows, value_rows, head_grad, *local_a), *near(*local_b[:2]), *far(local_b[2]))


def solution(mesh):
    rows = P("ctx", "head")
    return jax.shard_map(
        per_device,
        mesh=mesh,
        in_specs=(rows, rows, rows, rows, P("head", None)),
        out_specs=(rows, rows, rows),
        check_vma=False,
    )
```

```python
import functools
import math

import jax
import jax.numpy as jnp
import numpy as np
from jax import lax
from jax.experimental import pallas as pl
from jax.experimental.pallas import tpu as pltpu
from jax.sharding import PartitionSpec as P

HEAD = 128
BLOCK = 256
PAIR = 2 * HEAD
TILE = 256
F32, BF16 = jnp.float32, jnp.bfloat16
MIB = 1024 * 1024
IN_VMEM = pl.BlockSpec(memory_space=pltpu.VMEM)
ANYWHERE = pl.BlockSpec(memory_space=pl.ANY)


def near(*arrays):
    return [pltpu.with_memory_space_constraint(a, pltpu.VMEM) for a in arrays]


def far(*arrays):
    return [pltpu.with_memory_space_constraint(a, pltpu.HBM) for a in arrays]


def dot(a, b, contract):
    return lax.dot_general(a, b, (((contract[0],), (contract[1],)), ((), ())), preferred_element_type=F32)


def columns(j, size):
    return pl.ds(pl.multiple_of(j * size, size), size)


def spans(length):
    return [pl.ds(i * TILE, TILE) for i in range(length // TILE)]


def put_states(left, right, write):
    for h in range(0, left.shape[1] // HEAD, 2):
        both = slice(h * HEAD, (h + 2) * HEAD)
        product = dot(left[:, both], right[:, both], (0, 0)).astype(BF16)
        write(h, product[:HEAD, :HEAD])
        write(h + 1, product[HEAD:, HEAD:])


def first_kernel(mine_ref, grad_hbm, weight_hbm, key_hbm, value_hbm, part_ref, state_ref, there_ref,
                 grad_ref, here_ref, key_ref, value_ref, tile_sem, rest_sem):
    length, width = part_ref.shape
    rows = state_ref.shape[1]
    each = HEAD // rows
    tiles = spans(length)
    mine = mine_ref[0]
    grads, weights, keys, values = [
        [pltpu.make_async_copy(source.at[t, cols], target.at[t, :], tile_sem.at[n, i]) for i, t in enumerate(tiles)]
        for n, (source, target, cols) in enumerate(
            (
                (grad_hbm, grad_ref, slice(None)),
                (weight_hbm, here_ref, columns(mine, width)),
                (key_hbm, key_ref, slice(None)),
                (value_hbm, value_ref, slice(None)),
            )
        )
    ]
    rest = pltpu.make_async_copy(weight_hbm.at[:, columns(1 - mine, width)], there_ref, rest_sem)
    for copy in [grads[0], *weights, *grads[1:], *keys, *values, rest]:
        copy.start()
    for copy in weights:
        copy.wait()
    for copy, t in zip(grads, tiles):
        copy.wait()
        part_ref[t, :] = dot(grad_ref[t, :], here_ref[...], (1, 1))
    for copy in [*keys, *values]:
        copy.wait()

    def write(h, state):
        state_ref[h * each : (h + 1) * each] = state.reshape(each, rows, HEAD)

    put_states(key_ref, value_ref, write)
    rest.wait()


def second_kernel(grad_ref, weight_ref, part_ref, query_hbm, state_ref, head_hbm, sent_ref, query_ref, head_ref, sem, query_sem):
    rows = state_ref.shape[1]
    each = HEAD // rows
    fetch = pltpu.make_async_copy(query_hbm, query_ref, query_sem)
    fetch.start()
    copies = []
    for i, t in enumerate(spans(part_ref.shape[0])):
        head_ref[t, :] = (part_ref[t, :] + dot(grad_ref[t, :], weight_ref[...], (1, 1))).astype(BF16)
        copies.append(pltpu.make_async_copy(head_ref.at[t, :], head_hbm.at[t, :], sem.at[i]))
        copies[-1].start()
    sent_ref[:, 0] = state_ref[...]

    def write(h, state):
        sent_ref[h * each : (h + 1) * each, 1] = state.reshape(each, rows, HEAD)

    fetch.wait()
    put_states(query_ref, head_ref, write)
    for copy in copies:
        copy.wait()


def inner_kernel(factor, after_ref, query_ref, key_ref, value_ref, head_ref, dq_ref, dk_ref, dv_ref, *refs):
    del after_ref
    *rest, before_ref, behind_ref = refs
    blocks = query_ref.shape[0] // BLOCK
    down = lax.broadcasted_iota(jnp.int32, (BLOCK, BLOCK), 0)
    across = lax.broadcasted_iota(jnp.int32, (BLOCK, BLOCK), 1)
    left_head = lax.broadcasted_iota(jnp.int32, (PAIR, PAIR), 0) < HEAD
    same_head = left_head == (lax.broadcasted_iota(jnp.int32, (PAIR, PAIR), 1) < HEAD)
    parts = [pl.ds(b * BLOCK, BLOCK) for b in range(blocks)]

    def lowered(state):
        return jnp.where(same_head, factor * state, 0.0).astype(BF16)

    def scores(keep, left, right):
        return jnp.where(keep, factor * dot(left, right, (1, 1)), 0.0).astype(BF16)

    state = None
    for b in range(1, blocks):
        step = dot(key_ref[parts[b - 1], :], value_ref[parts[b - 1], :], (0, 0))
        state = step if state is None else state + step
        before_ref[b] = lowered(state)
    state = None
    for b in reversed(range(blocks - 1)):
        step = dot(query_ref[parts[b + 1], :], head_ref[parts[b + 1], :], (0, 0))
        state = step if state is None else state + step
        behind_ref[b] = lowered(state)
    for b, at in enumerate(parts):
        sums = [None] * 3
        if b > 0:
            sums[0] = dot(head_ref[at, :], before_ref[b], (1, 1))
        if b < blocks - 1:
            low = behind_ref[b]
            sums[1:] = dot(value_ref[at, :], low, (1, 1)), dot(key_ref[at, :], low, (1, 0))
        for h in range(2):
            col = slice(h * HEAD, (h + 1) * HEAD)
            q, k, v, g = query_ref[at, col], key_ref[at, col], value_ref[at, col], head_ref[at, col]
            values = [
                dot(scores(across <= down, g, v), k, (1, 0)),
                dot(scores(down <= across, v, g), q, (1, 0)),
                dot(scores(down <= across, k, q), g, (1, 0)),
            ]
            for ref, value, extra in zip((dq_ref, dk_ref, dv_ref), values, sums):
                if extra is not None:
                    value = value + extra[:, col]
                out = col if ref.shape[1] == PAIR else columns(2 * pl.program_id(0) + h, HEAD)
                value, inside = value.astype(BF16), min(BLOCK, ref.shape[0] - b * BLOCK)
                ref[pl.ds(b * BLOCK, inside), out] = value[:inside]
                if inside < BLOCK:
                    rest[0][:, col] = value[inside:]


def middle_kernel(factor, place, given_ref, after_ref, carried_ref):
    del after_ref
    count, _, rows, width = given_ref.shape
    for which, devices in ((0, place), (1, place[::-1])):
        total = jnp.zeros((rows, width), F32)
        for i in devices:
            carried_ref[i, which] = (factor * total).astype(BF16)
            total = total + given_ref[i, which].astype(F32)


def two_heads(carried_ref, h, which):
    each = HEAD // carried_ref.shape[2]
    one = carried_ref[h * each : (h + 1) * each, which].reshape(HEAD, HEAD)
    two = carried_ref[(h + 1) * each : (h + 2) * each, which].reshape(HEAD, HEAD)
    none = jnp.zeros_like(one)
    return jnp.concatenate([jnp.concatenate([one, none], 1), jnp.concatenate([none, two], 1)], 0)


def last_kernel(carried_ref, key_hbm, value_hbm, head_hbm, dq_a, dk_a, dv_a, dq_b, dk_b, dv_b, dv_tail, dq_hbm, dk_hbm, dv_hbm, *refs):
    inputs, outputs, (sem, out_sem) = refs[:7], refs[7:10], refs[10:]
    sources, targets = (head_hbm, dq_a, value_hbm, dk_a, key_hbm, dv_a), (dq_hbm, dk_hbm, dv_hbm)
    near_rows = dv_b.shape[0]
    length, width = outputs[0].shape
    edges = [0, TILE // 2, *range(TILE // 2 + TILE, length, TILE), length]
    tiles = [pl.ds(a, b - a) for a, b in zip(edges, edges[1:])]
    loads = [
        [pltpu.make_async_copy(a.at[t, :], b.at[t, :], sem.at[n, i]) for n, (a, b) in enumerate(zip(sources, inputs))]
        for i, t in enumerate(tiles)
    ]
    loads[-1].append(pltpu.make_async_copy(dv_tail, inputs[6], sem.at[6, 0]))
    stores = [
        [pltpu.make_async_copy(a.at[t, :], b.at[t, :], out_sem.at[n, i]) for n, (a, b) in enumerate(zip(outputs, targets))]
        for i, t in enumerate(tiles)
    ]
    for copy in sum(loads, []):
        copy.start()
    states = [(two_heads(carried_ref, h, 0), two_heads(carried_ref, h, 1)) for h in range(0, width // HEAD, 2)]
    half = width // 2
    grads, dq_in, values, dk_in, keys, dv_in, dv_rest = inputs
    for i, t in enumerate(tiles):
        for copy in loads[i]:
            copy.wait()
        for j, (before, after) in enumerate(states):
            col = slice(j * PAIR, (j + 1) * PAIR)
            if j * PAIR < half:
                locals_ = dq_in[t, col], dk_in[t, col], dv_in[t, col]
            else:
                low = slice(j * PAIR - half, (j + 1) * PAIR - half)
                last = edges[i] == near_rows
                locals_ = dq_b[t, low], dk_b[t, low], dv_rest[:, low] if last else dv_b[t, low]
            sums = dot(grads[t, col], before, (1, 1)), dot(values[t, col], after, (1, 1)), dot(keys[t, col], after, (1, 0))
            for ref, own, carried in zip(outputs, locals_, sums):
                ref[t, col] = (own + carried).astype(BF16)
        for copy in stores[i]:
            copy.start()
    for copy in sum(stores, []):
        copy.wait()


def per_device(query_rows, key_rows, value_rows, out_grad, out_weight):
    length, width = query_rows.shape
    count = lax.axis_size("ctx")
    order = [count - 1, *(int(i) for i in np.random.default_rng(0).permutation(count - 1))]
    place = [order.index(i) for i in range(count)]
    heads = width // HEAD
    factor = 1.0 / math.sqrt(HEAD * length * count)
    rows = width // count
    params = pltpu.CompilerParams(vmem_limit_bytes=16 * MIB)
    product = 2 * length * width * width
    area = length * width

    def cost(flops, bytes_accessed):
        return pl.CostEstimate(flops=int(flops), bytes_accessed=int(bytes_accessed), transcendentals=0)

    other_grad = lax.ppermute(out_grad, "head", [(0, 1), (1, 0)])
    mine = lax.axis_index("head").astype(jnp.int32).reshape(1)

    semaphores = pltpu.SemaphoreType.DMA
    tiles = length // TILE
    part, key_state, there = pl.pallas_call(
        first_kernel,
        in_specs=[pl.BlockSpec(memory_space=pltpu.SMEM)] + [ANYWHERE] * 4,
        out_specs=[IN_VMEM] * 3,
        out_shape=[
            pltpu.VMEM((length, width), F32),
            jax.ShapeDtypeStruct((count, rows, HEAD), BF16),
            pltpu.VMEM((width, width), BF16),
        ],
        scratch_shapes=[pltpu.VMEM((length, width), BF16)] * 4 + [semaphores((4, tiles)), semaphores],
        compiler_params=params,
        cost_estimate=cost(2 * product, 12 * area),
        name="own_part",
    )(mine, *far(out_grad, out_weight, key_rows, value_rows))

    head_grad, sent = pl.pallas_call(
        second_kernel,
        in_specs=[IN_VMEM] * 3 + [ANYWHERE, IN_VMEM],
        out_specs=[ANYWHERE, IN_VMEM],
        out_shape=[pltpu.HBM((length, width), BF16), pltpu.VMEM((count, 2, rows, HEAD), BF16)],
        scratch_shapes=[pltpu.VMEM((length, width), BF16)] * 2 + [semaphores((tiles,)), semaphores],
        compiler_params=params,
        cost_estimate=cost(2 * product, 8 * area),
        name="other_part",
    )(*near(other_grad, there, part), *far(query_rows), *near(key_state))

    given = lax.all_to_all(sent, "ctx", 0, 0, axis_index_groups=[order])

    def inner(base, number, after, near_rows):
        shapes, specs = [], []
        for top in near_rows:
            shapes.append(pltpu.VMEM((top, number * HEAD), BF16) if top else pltpu.HBM((length, number * HEAD), BF16))
            specs.append(IN_VMEM if top else pl.BlockSpec((length, PAIR), lambda h: (0, h)))
        if 0 < near_rows[2] < length:
            shapes.append(pltpu.HBM((length - near_rows[2], number * HEAD), BF16))
            specs.append(pl.BlockSpec((length - near_rows[2], PAIR), lambda h: (0, h)))
        return pl.pallas_call(
            functools.partial(inner_kernel, factor),
            grid=(number // 2,),
            in_specs=[ANYWHERE] + [pl.BlockSpec((length, PAIR), lambda h: (0, h + base // 2))] * 4,
            out_specs=specs,
            out_shape=shapes,
            scratch_shapes=[pltpu.VMEM((length // BLOCK, PAIR, PAIR), BF16)] * 2,
            compiler_params=params,
            cost_estimate=cost(6 * product * number / heads, 10 * area),
            name=f"inner_{base}",
        )(after, *far(query_rows, key_rows, value_rows, head_grad))

    half = heads // 2
    local_a = inner(0, half, key_state, (0, 0, 0))
    carried = pl.pallas_call(
        functools.partial(middle_kernel, factor, place),
        in_specs=[IN_VMEM, ANYWHERE],
        out_specs=IN_VMEM,
        out_shape=pltpu.VMEM(given.shape, BF16),
        compiler_params=pltpu.CompilerParams(vmem_limit_bytes=4 * MIB),
        name="sums",
    )(*near(given), *far(local_a[0]))
    local_b = inner(half, heads - half, carried, (length, length, length - TILE // 2))
    carried = lax.all_to_all(carried, "ctx", 0, 0, axis_index_groups=[order])

    full, part_width = pltpu.VMEM((length, width), BF16), pltpu.VMEM((length, width // 2), BF16)
    tail = pltpu.VMEM((TILE // 2, width // 2), BF16)
    steps = tiles + 1
    return pl.pallas_call(
        last_kernel,
        in_specs=[IN_VMEM] + [ANYWHERE] * 6 + [IN_VMEM] * 3 + [ANYWHERE],
        out_specs=[ANYWHERE] * 3,
        out_shape=[jax.ShapeDtypeStruct((length, width), BF16)] * 3,
        scratch_shapes=[full, part_width, full, part_width, full, part_width, tail, full, full, full]
        + [semaphores((7, steps)), semaphores((3, steps))],
        compiler_params=pltpu.CompilerParams(vmem_limit_bytes=24 * MIB),
        cost_estimate=cost(product, 18 * area),
        name="carried_part",
    )(*near(carried), *far(key_rows, value_rows, head_grad, *local_a), *near(*local_b[:3]), *far(local_b[3]))


def solution(mesh):
    rows = P("ctx", "head")
    return jax.shard_map(
        per_device,
        mesh=mesh,
        in_specs=(rows, rows, rows, rows, P("head", None)),
        out_specs=(rows, rows, rows),
        check_vma=False,
    )
```

```python
import functools
import math

import jax
import jax.numpy as jnp
import numpy as np
from jax import lax
from jax.experimental import pallas as pl
from jax.experimental.pallas import tpu as pltpu
from jax.sharding import PartitionSpec as P

HEAD = 128
BLOCK = 256
PAIR = 2 * HEAD
TILE = 256
F32, BF16 = jnp.float32, jnp.bfloat16
MIB = 1024 * 1024
IN_VMEM = pl.BlockSpec(memory_space=pltpu.VMEM)
ANYWHERE = pl.BlockSpec(memory_space=pl.ANY)


def near(*arrays):
    return [pltpu.with_memory_space_constraint(a, pltpu.VMEM) for a in arrays]


def far(*arrays):
    return [pltpu.with_memory_space_constraint(a, pltpu.HBM) for a in arrays]


def dot(a, b, contract):
    return lax.dot_general(a, b, (((contract[0],), (contract[1],)), ((), ())), preferred_element_type=F32)


def columns(j, size):
    return pl.ds(pl.multiple_of(j * size, size), size)


def spans(length):
    return [pl.ds(i * TILE, TILE) for i in range(length // TILE)]


def put_states(left, right, write):
    for h in range(0, left.shape[1] // HEAD, 2):
        both = slice(h * HEAD, (h + 2) * HEAD)
        product = dot(left[:, both], right[:, both], (0, 0)).astype(BF16)
        write(h, product[:HEAD, :HEAD])
        write(h + 1, product[HEAD:, HEAD:])


def first_kernel(mine_ref, grad_hbm, weight_hbm, key_hbm, value_hbm, part_ref, state_ref, there_ref,
                 grad_ref, here_ref, key_ref, value_ref, tile_sem, rest_sem):
    length, width = part_ref.shape
    rows = state_ref.shape[1]
    each = HEAD // rows
    tiles = spans(length)
    mine = mine_ref[0]
    grads, weights, keys, values = [
        [pltpu.make_async_copy(source.at[t, cols], target.at[t, :], tile_sem.at[n, i]) for i, t in enumerate(tiles)]
        for n, (source, target, cols) in enumerate(
            (
                (grad_hbm, grad_ref, slice(None)),
                (weight_hbm, here_ref, columns(mine, width)),
                (key_hbm, key_ref, slice(None)),
                (value_hbm, value_ref, slice(None)),
            )
        )
    ]
    rest = pltpu.make_async_copy(weight_hbm.at[:, columns(1 - mine, width)], there_ref, rest_sem)
    for copy in [grads[0], *weights, *grads[1:], *keys, *values, rest]:
        copy.start()
    for copy in weights:
        copy.wait()
    for copy, t in zip(grads, tiles):
        copy.wait()
        part_ref[t, :] = dot(grad_ref[t, :], here_ref[...], (1, 1))
    for copy in [*keys, *values]:
        copy.wait()

    def write(h, state):
        state_ref[h * each : (h + 1) * each] = state.reshape(each, rows, HEAD)

    put_states(key_ref, value_ref, write)
    rest.wait()


def second_kernel(grad_ref, weight_ref, part_ref, query_hbm, state_ref, head_hbm, sent_ref, query_ref, head_ref, sem, query_sem):
    rows = state_ref.shape[1]
    each = HEAD // rows
    fetch = pltpu.make_async_copy(query_hbm, query_ref, query_sem)
    fetch.start()
    copies = []
    for i, t in enumerate(spans(part_ref.shape[0])):
        head_ref[t, :] = (part_ref[t, :] + dot(grad_ref[t, :], weight_ref[...], (1, 1))).astype(BF16)
        copies.append(pltpu.make_async_copy(head_ref.at[t, :], head_hbm.at[t, :], sem.at[i]))
        copies[-1].start()
    sent_ref[:, 0] = state_ref[...]

    def write(h, state):
        sent_ref[h * each : (h + 1) * each, 1] = state.reshape(each, rows, HEAD)

    fetch.wait()
    put_states(query_ref, head_ref, write)
    for copy in copies:
        copy.wait()


def inner_kernel(factor, after_ref, query_ref, key_ref, value_ref, head_ref, dq_ref, dk_ref, dv_ref, *refs):
    del after_ref
    *rest, before_ref, behind_ref = refs
    blocks = query_ref.shape[0] // BLOCK
    down = lax.broadcasted_iota(jnp.int32, (BLOCK, BLOCK), 0)
    across = lax.broadcasted_iota(jnp.int32, (BLOCK, BLOCK), 1)
    left_head = lax.broadcasted_iota(jnp.int32, (PAIR, PAIR), 0) < HEAD
    same_head = left_head == (lax.broadcasted_iota(jnp.int32, (PAIR, PAIR), 1) < HEAD)
    parts = [pl.ds(b * BLOCK, BLOCK) for b in range(blocks)]

    def lowered(state):
        return jnp.where(same_head, factor * state, 0.0).astype(BF16)

    def scores(keep, left, right):
        return jnp.where(keep, factor * dot(left, right, (1, 1)), 0.0).astype(BF16)

    state = None
    for b in range(1, blocks):
        step = dot(key_ref[parts[b - 1], :], value_ref[parts[b - 1], :], (0, 0))
        state = step if state is None else state + step
        before_ref[b] = lowered(state)
    state = None
    for b in reversed(range(blocks - 1)):
        step = dot(query_ref[parts[b + 1], :], head_ref[parts[b + 1], :], (0, 0))
        state = step if state is None else state + step
        behind_ref[b] = lowered(state)
    for b, at in enumerate(parts):
        sums = [None] * 3
        if b > 0:
            sums[0] = dot(head_ref[at, :], before_ref[b], (1, 1))
        if b < blocks - 1:
            low = behind_ref[b]
            sums[1:] = dot(value_ref[at, :], low, (1, 1)), dot(key_ref[at, :], low, (1, 0))
        for h in range(2):
            col = slice(h * HEAD, (h + 1) * HEAD)
            q, k, v, g = query_ref[at, col], key_ref[at, col], value_ref[at, col], head_ref[at, col]
            values = [
                dot(scores(across <= down, g, v), k, (1, 0)),
                dot(scores(down <= across, v, g), q, (1, 0)),
                dot(scores(down <= across, k, q), g, (1, 0)),
            ]
            for ref, value, extra in zip((dq_ref, dk_ref, dv_ref), values, sums):
                if extra is not None:
                    value = value + extra[:, col]
                out = col if ref.shape[1] == PAIR else columns(2 * pl.program_id(0) + h, HEAD)
                value, inside = value.astype(BF16), min(BLOCK, ref.shape[0] - b * BLOCK)
                ref[pl.ds(b * BLOCK, inside), out] = value[:inside]
                if inside < BLOCK:
                    rest[0][:, col] = value[inside:]


def middle_kernel(factor, place, given_ref, after_ref, carried_ref):
    del after_ref
    count, _, rows, width = given_ref.shape
    for which, devices in ((0, place), (1, place[::-1])):
        total = jnp.zeros((rows, width), F32)
        for i in devices:
            carried_ref[i, which] = (factor * total).astype(BF16)
            total = total + given_ref[i, which].astype(F32)


def two_heads(carried_ref, h, which):
    each = HEAD // carried_ref.shape[2]
    one = carried_ref[h * each : (h + 1) * each, which].reshape(HEAD, HEAD)
    two = carried_ref[(h + 1) * each : (h + 2) * each, which].reshape(HEAD, HEAD)
    none = jnp.zeros_like(one)
    return jnp.concatenate([jnp.concatenate([one, none], 1), jnp.concatenate([none, two], 1)], 0)


def last_kernel(carried_ref, key_hbm, value_hbm, head_hbm, dq_a, dk_a, dv_a, dq_b, dk_b, dv_b, dv_tail, dq_hbm, dk_hbm, dv_hbm, *refs):
    inputs, outputs, (sem, out_sem) = refs[:7], refs[7:10], refs[10:]
    sources, targets = (head_hbm, dq_a, value_hbm, dk_a, key_hbm, dv_a), (dq_hbm, dk_hbm, dv_hbm)
    near_rows = dv_b.shape[0]
    length, width = outputs[0].shape
    edges = [0, TILE // 2, *range(TILE // 2 + TILE, length, TILE), length]
    tiles = [pl.ds(a, b - a) for a, b in zip(edges, edges[1:])]
    loads = [
        [pltpu.make_async_copy(a.at[t, :], b.at[t, :], sem.at[n, i]) for n, (a, b) in enumerate(zip(sources, inputs))]
        for i, t in enumerate(tiles)
    ]
    loads[-1].append(pltpu.make_async_copy(dv_tail, inputs[6], sem.at[6, 0]))
    stores = [
        [pltpu.make_async_copy(a.at[t, :], b.at[t, :], out_sem.at[n, i]) for n, (a, b) in enumerate(zip(outputs, targets))]
        for i, t in enumerate(tiles)
    ]
    for copy in sum(loads, []):
        copy.start()
    states = [(two_heads(carried_ref, h, 0), two_heads(carried_ref, h, 1)) for h in range(0, width // HEAD, 2)]
    half = width // 2
    grads, dq_in, values, dk_in, keys, dv_in, dv_rest = inputs
    for i, t in enumerate(tiles):
        last = edges[i] == near_rows
        results = (
            (grads, dq_in, dq_b, 0, 1, loads[i][:2]),
            (values, dk_in, dk_b, 1, 1, loads[i][2:4]),
            (keys, dv_in, dv_rest if last else dv_b, 1, 0, loads[i][4:]),
        )
        for n, (rows, own_a, own_b, which, side, needed) in enumerate(results):
            for copy in needed:
                copy.wait()
            for j, pair in enumerate(states):
                col = slice(j * PAIR, (j + 1) * PAIR)
                if j * PAIR < half:
                    own = own_a[t, col]
                else:
                    low = slice(j * PAIR - half, (j + 1) * PAIR - half)
                    own = own_b[:, low] if own_b is dv_rest else own_b[t, low]
                outputs[n][t, col] = (own + dot(rows[t, col], pair[which], (1, side))).astype(BF16)
            stores[i][n].start()
    for copy in sum(stores, []):
        copy.wait()


def per_device(query_rows, key_rows, value_rows, out_grad, out_weight):
    length, width = query_rows.shape
    count = lax.axis_size("ctx")
    order = [count - 1, *(int(i) for i in np.random.default_rng(0).permutation(count - 1))]
    place = [order.index(i) for i in range(count)]
    heads = width // HEAD
    factor = 1.0 / math.sqrt(HEAD * length * count)
    rows = width // count
    params = pltpu.CompilerParams(vmem_limit_bytes=16 * MIB)
    product = 2 * length * width * width
    area = length * width

    def cost(flops, bytes_accessed):
        return pl.CostEstimate(flops=int(flops), bytes_accessed=int(bytes_accessed), transcendentals=0)

    other_grad = lax.ppermute(out_grad, "head", [(0, 1), (1, 0)])
    mine = lax.axis_index("head").astype(jnp.int32).reshape(1)

    semaphores = pltpu.SemaphoreType.DMA
    tiles = length // TILE
    part, key_state, there = pl.pallas_call(
        first_kernel,
        in_specs=[pl.BlockSpec(memory_space=pltpu.SMEM)] + [ANYWHERE] * 4,
        out_specs=[IN_VMEM] * 3,
        out_shape=[
            pltpu.VMEM((length, width), F32),
            jax.ShapeDtypeStruct((count, rows, HEAD), BF16),
            pltpu.VMEM((width, width), BF16),
        ],
        scratch_shapes=[pltpu.VMEM((length, width), BF16)] * 4 + [semaphores((4, tiles)), semaphores],
        compiler_params=params,
        cost_estimate=cost(2 * product, 12 * area),
        name="own_part",
    )(mine, *far(out_grad, out_weight, key_rows, value_rows))

    head_grad, sent = pl.pallas_call(
        second_kernel,
        in_specs=[IN_VMEM] * 3 + [ANYWHERE, IN_VMEM],
        out_specs=[ANYWHERE, IN_VMEM],
        out_shape=[pltpu.HBM((length, width), BF16), pltpu.VMEM((count, 2, rows, HEAD), BF16)],
        scratch_shapes=[pltpu.VMEM((length, width), BF16)] * 2 + [semaphores((tiles,)), semaphores],
        compiler_params=params,
        cost_estimate=cost(2 * product, 8 * area),
        name="other_part",
    )(*near(other_grad, there, part), *far(query_rows), *near(key_state))

    given = lax.all_to_all(sent, "ctx", 0, 0, axis_index_groups=[order])

    def inner(base, number, after, near_rows):
        shapes, specs = [], []
        for top in near_rows:
            shapes.append(pltpu.VMEM((top, number * HEAD), BF16) if top else pltpu.HBM((length, number * HEAD), BF16))
            specs.append(IN_VMEM if top else pl.BlockSpec((length, PAIR), lambda h: (0, h)))
        if 0 < near_rows[2] < length:
            shapes.append(pltpu.HBM((length - near_rows[2], number * HEAD), BF16))
            specs.append(pl.BlockSpec((length - near_rows[2], PAIR), lambda h: (0, h)))
        return pl.pallas_call(
            functools.partial(inner_kernel, factor),
            grid=(number // 2,),
            in_specs=[ANYWHERE] + [pl.BlockSpec((length, PAIR), lambda h: (0, h + base // 2))] * 4,
            out_specs=specs,
            out_shape=shapes,
            scratch_shapes=[pltpu.VMEM((length // BLOCK, PAIR, PAIR), BF16)] * 2,
            compiler_params=params,
            cost_estimate=cost(6 * product * number / heads, 10 * area),
            name=f"inner_{base}",
        )(after, *far(query_rows, key_rows, value_rows, head_grad))

    half = heads // 2
    local_a = inner(0, half, key_state, (0, 0, 0))
    carried = pl.pallas_call(
        functools.partial(middle_kernel, factor, place),
        in_specs=[IN_VMEM, ANYWHERE],
        out_specs=IN_VMEM,
        out_shape=pltpu.VMEM(given.shape, BF16),
        compiler_params=pltpu.CompilerParams(vmem_limit_bytes=4 * MIB),
        name="sums",
    )(*near(given), *far(local_a[0]))
    local_b = inner(half, heads - half, carried, (length, length, length - TILE // 2))
    carried = lax.all_to_all(carried, "ctx", 0, 0, axis_index_groups=[order])

    full, part_width = pltpu.VMEM((length, width), BF16), pltpu.VMEM((length, width // 2), BF16)
    tail = pltpu.VMEM((TILE // 2, width // 2), BF16)
    steps = tiles + 1
    return pl.pallas_call(
        last_kernel,
        in_specs=[IN_VMEM] + [ANYWHERE] * 6 + [IN_VMEM] * 3 + [ANYWHERE],
        out_specs=[ANYWHERE] * 3,
        out_shape=[jax.ShapeDtypeStruct((length, width), BF16)] * 3,
        scratch_shapes=[full, part_width, full, part_width, full, part_width, tail, full, full, full]
        + [semaphores((7, steps)), semaphores((3, steps))],
        compiler_params=pltpu.CompilerParams(vmem_limit_bytes=24 * MIB),
        cost_estimate=cost(product, 18 * area),
        name="carried_part",
    )(*near(carried), *far(key_rows, value_rows, head_grad, *local_a), *near(*local_b[:3]), *far(local_b[3]))


def solution(mesh):
    rows = P("ctx", "head")
    return jax.shard_map(
        per_device,
        mesh=mesh,
        in_specs=(rows, rows, rows, rows, P("head", None)),
        out_specs=(rows, rows, rows),
        check_vma=False,
    )
```

```python
import functools
import math

import jax
import jax.numpy as jnp
import numpy as np
from jax import lax
from jax.experimental import pallas as pl
from jax.experimental.pallas import tpu as pltpu
from jax.sharding import PartitionSpec as P

HEAD = 128
BLOCK = 256
PAIR = 2 * HEAD
TILE = 256
F32, BF16 = jnp.float32, jnp.bfloat16
MIB = 1024 * 1024
IN_VMEM = pl.BlockSpec(memory_space=pltpu.VMEM)
ANYWHERE = pl.BlockSpec(memory_space=pl.ANY)


def near(*arrays):
    return [pltpu.with_memory_space_constraint(a, pltpu.VMEM) for a in arrays]


def far(*arrays):
    return [pltpu.with_memory_space_constraint(a, pltpu.HBM) for a in arrays]


def dot(a, b, contract):
    return lax.dot_general(a, b, (((contract[0],), (contract[1],)), ((), ())), preferred_element_type=F32)


def columns(j, size):
    return pl.ds(pl.multiple_of(j * size, size), size)


def spans(length):
    return [pl.ds(i * TILE, TILE) for i in range(length // TILE)]


def put_states(left, right, write):
    for h in range(0, left.shape[1] // HEAD, 2):
        both = slice(h * HEAD, (h + 2) * HEAD)
        product = dot(left[:, both], right[:, both], (0, 0)).astype(BF16)
        write(h, product[:HEAD, :HEAD])
        write(h + 1, product[HEAD:, HEAD:])


def first_kernel(mine_ref, grad_hbm, weight_hbm, key_hbm, value_hbm, part_ref, state_ref, there_ref,
                 grad_ref, here_ref, key_ref, value_ref, tile_sem, rest_sem):
    length, width = part_ref.shape
    rows = state_ref.shape[1]
    each = HEAD // rows
    tiles = spans(length)
    mine = mine_ref[0]
    grads, weights, keys, values = [
        [pltpu.make_async_copy(source.at[t, cols], target.at[t, :], tile_sem.at[n, i]) for i, t in enumerate(tiles)]
        for n, (source, target, cols) in enumerate(
            (
                (grad_hbm, grad_ref, slice(None)),
                (weight_hbm, here_ref, columns(mine, width)),
                (key_hbm, key_ref, slice(None)),
                (value_hbm, value_ref, slice(None)),
            )
        )
    ]
    rest = pltpu.make_async_copy(weight_hbm.at[:, columns(1 - mine, width)], there_ref, rest_sem)
    for copy in [grads[0], *weights, *grads[1:], *keys, *values, rest]:
        copy.start()
    for copy in weights:
        copy.wait()
    for copy, t in zip(grads, tiles):
        copy.wait()
        part_ref[t, :] = dot(grad_ref[t, :], here_ref[...], (1, 1))
    for copy in [*keys, *values]:
        copy.wait()

    def write(h, state):
        state_ref[h * each : (h + 1) * each] = state.reshape(each, rows, HEAD)

    put_states(key_ref, value_ref, write)
    rest.wait()


def second_kernel(grad_ref, weight_ref, part_ref, query_hbm, state_ref, head_hbm, sent_hbm,
                  query_ref, head_ref, sent_ref, sem, query_sem, sent_sem):
    rows = state_ref.shape[1]
    each = HEAD // rows
    fetch = pltpu.make_async_copy(query_hbm, query_ref, query_sem)
    fetch.start()
    copies = []
    for i, t in enumerate(spans(part_ref.shape[0])):
        head_ref[t, :] = (part_ref[t, :] + dot(grad_ref[t, :], weight_ref[...], (1, 1))).astype(BF16)
        copies.append(pltpu.make_async_copy(head_ref.at[t, :], head_hbm.at[t, :], sem.at[i]))
        copies[-1].start()
    sent_ref[:, 0] = state_ref[...]

    def write(h, state):
        sent_ref[h * each : (h + 1) * each, 1] = state.reshape(each, rows, HEAD)
        if h % 2:
            both = pl.ds((h - 1) * each, 2 * each)
            copies.append(pltpu.make_async_copy(sent_ref.at[both], sent_hbm.at[both], sent_sem.at[h // 2]))
            copies[-1].start()

    fetch.wait()
    put_states(query_ref, head_ref, write)
    for copy in copies:
        copy.wait()


def inner_kernel(factor, after_ref, query_ref, key_ref, value_ref, head_ref, dq_ref, dk_ref, dv_ref, *refs):
    del after_ref
    *rest, before_ref, behind_ref = refs
    blocks = query_ref.shape[0] // BLOCK
    down = lax.broadcasted_iota(jnp.int32, (BLOCK, BLOCK), 0)
    across = lax.broadcasted_iota(jnp.int32, (BLOCK, BLOCK), 1)
    left_head = lax.broadcasted_iota(jnp.int32, (PAIR, PAIR), 0) < HEAD
    same_head = left_head == (lax.broadcasted_iota(jnp.int32, (PAIR, PAIR), 1) < HEAD)
    parts = [pl.ds(b * BLOCK, BLOCK) for b in range(blocks)]

    def lowered(state):
        return jnp.where(same_head, factor * state, 0.0).astype(BF16)

    def scores(keep, left, right):
        return jnp.where(keep, factor * dot(left, right, (1, 1)), 0.0).astype(BF16)

    state = None
    for b in range(1, blocks):
        step = dot(key_ref[parts[b - 1], :], value_ref[parts[b - 1], :], (0, 0))
        state = step if state is None else state + step
        before_ref[b] = lowered(state)
    state = None
    for b in reversed(range(blocks - 1)):
        step = dot(query_ref[parts[b + 1], :], head_ref[parts[b + 1], :], (0, 0))
        state = step if state is None else state + step
        behind_ref[b] = lowered(state)
    for b, at in enumerate(parts):
        sums = [None] * 3
        if b > 0:
            sums[0] = dot(head_ref[at, :], before_ref[b], (1, 1))
        if b < blocks - 1:
            low = behind_ref[b]
            sums[1:] = dot(value_ref[at, :], low, (1, 1)), dot(key_ref[at, :], low, (1, 0))
        for h in range(2):
            col = slice(h * HEAD, (h + 1) * HEAD)
            q, k, v, g = query_ref[at, col], key_ref[at, col], value_ref[at, col], head_ref[at, col]
            values = [
                dot(scores(across <= down, g, v), k, (1, 0)),
                dot(scores(down <= across, v, g), q, (1, 0)),
                dot(scores(down <= across, k, q), g, (1, 0)),
            ]
            for ref, value, extra in zip((dq_ref, dk_ref, dv_ref), values, sums):
                if extra is not None:
                    value = value + extra[:, col]
                out = col if ref.shape[1] == PAIR else columns(2 * pl.program_id(0) + h, HEAD)
                value, inside = value.astype(BF16), min(BLOCK, ref.shape[0] - b * BLOCK)
                ref[pl.ds(b * BLOCK, inside), out] = value[:inside]
                if inside < BLOCK:
                    rest[0][:, col] = value[inside:]


def middle_kernel(factor, place, given_ref, after_ref, carried_ref):
    del after_ref
    count, _, rows, width = given_ref.shape
    for which, devices in ((0, place), (1, place[::-1])):
        total = jnp.zeros((rows, width), F32)
        for i in devices:
            carried_ref[i, which] = (factor * total).astype(BF16)
            total = total + given_ref[i, which].astype(F32)


def two_heads(carried_ref, h, which):
    each = HEAD // carried_ref.shape[2]
    one = carried_ref[h * each : (h + 1) * each, which].reshape(HEAD, HEAD)
    two = carried_ref[(h + 1) * each : (h + 2) * each, which].reshape(HEAD, HEAD)
    none = jnp.zeros_like(one)
    return jnp.concatenate([jnp.concatenate([one, none], 1), jnp.concatenate([none, two], 1)], 0)


def last_kernel(carried_ref, key_hbm, value_hbm, head_hbm, dq_a, dk_a, dv_a, dq_b, dk_b, dv_b, dv_tail, dq_hbm, dk_hbm, dv_hbm, *refs):
    inputs, outputs, (sem, out_sem) = refs[:7], refs[7:10], refs[10:]
    sources, targets = (head_hbm, dq_a, value_hbm, dk_a, key_hbm, dv_a), (dq_hbm, dk_hbm, dv_hbm)
    near_rows = dv_b.shape[0]
    length, width = outputs[0].shape
    edges = [0, TILE // 2, *range(TILE // 2 + TILE, length, TILE), length]
    tiles = [pl.ds(a, b - a) for a, b in zip(edges, edges[1:])]
    loads = [
        [pltpu.make_async_copy(a.at[t, :], b.at[t, :], sem.at[n, i]) for n, (a, b) in enumerate(zip(sources, inputs))]
        for i, t in enumerate(tiles)
    ]
    loads[-1].append(pltpu.make_async_copy(dv_tail, inputs[6], sem.at[6, 0]))
    stores = [
        [pltpu.make_async_copy(a.at[t, :], b.at[t, :], out_sem.at[n, i]) for n, (a, b) in enumerate(zip(outputs, targets))]
        for i, t in enumerate(tiles)
    ]
    for copy in sum(loads, []):
        copy.start()
    states = [(two_heads(carried_ref, h, 0), two_heads(carried_ref, h, 1)) for h in range(0, width // HEAD, 2)]
    half = width // 2
    grads, dq_in, values, dk_in, keys, dv_in, dv_rest = inputs
    for i, t in enumerate(tiles):
        last = edges[i] == near_rows
        results = (
            (grads, dq_in, dq_b, 0, 1, loads[i][:2]),
            (values, dk_in, dk_b, 1, 1, loads[i][2:4]),
            (keys, dv_in, dv_rest if last else dv_b, 1, 0, loads[i][4:]),
        )
        for n, (rows, own_a, own_b, which, side, needed) in enumerate(results):
            for copy in needed:
                copy.wait()
            for j, pair in enumerate(states):
                col = slice(j * PAIR, (j + 1) * PAIR)
                if j * PAIR < half:
                    own = own_a[t, col]
                else:
                    low = slice(j * PAIR - half, (j + 1) * PAIR - half)
                    own = own_b[:, low] if own_b is dv_rest else own_b[t, low]
                outputs[n][t, col] = (own + dot(rows[t, col], pair[which], (1, side))).astype(BF16)
            stores[i][n].start()
    for copy in sum(stores, []):
        copy.wait()


def per_device(query_rows, key_rows, value_rows, out_grad, out_weight):
    length, width = query_rows.shape
    count = lax.axis_size("ctx")
    order = [count - 1, *(int(i) for i in np.random.default_rng(0).permutation(count - 1))]
    place = [order.index(i) for i in range(count)]
    heads = width // HEAD
    factor = 1.0 / math.sqrt(HEAD * length * count)
    rows = width // count
    params = pltpu.CompilerParams(vmem_limit_bytes=16 * MIB)
    product = 2 * length * width * width
    area = length * width

    def cost(flops, bytes_accessed):
        return pl.CostEstimate(flops=int(flops), bytes_accessed=int(bytes_accessed), transcendentals=0)

    other_grad = lax.ppermute(out_grad, "head", [(0, 1), (1, 0)])
    mine = lax.axis_index("head").astype(jnp.int32).reshape(1)

    semaphores = pltpu.SemaphoreType.DMA
    tiles = length // TILE
    part, key_state, there = pl.pallas_call(
        first_kernel,
        in_specs=[pl.BlockSpec(memory_space=pltpu.SMEM)] + [ANYWHERE] * 4,
        out_specs=[IN_VMEM] * 3,
        out_shape=[
            pltpu.VMEM((length, width), F32),
            jax.ShapeDtypeStruct((count, rows, HEAD), BF16),
            pltpu.VMEM((width, width), BF16),
        ],
        scratch_shapes=[pltpu.VMEM((length, width), BF16)] * 4 + [semaphores((4, tiles)), semaphores],
        compiler_params=params,
        cost_estimate=cost(2 * product, 12 * area),
        name="own_part",
    )(mine, *far(out_grad, out_weight, key_rows, value_rows))

    head_grad, sent = pl.pallas_call(
        second_kernel,
        in_specs=[IN_VMEM] * 3 + [ANYWHERE, IN_VMEM],
        out_specs=[ANYWHERE, ANYWHERE],
        out_shape=[pltpu.HBM((length, width), BF16), pltpu.HBM((count, 2, rows, HEAD), BF16)],
        scratch_shapes=[pltpu.VMEM((length, width), BF16)] * 2
        + [pltpu.VMEM((count, 2, rows, HEAD), BF16)]
        + [semaphores((tiles,)), semaphores, semaphores((heads // 2,))],
        compiler_params=params,
        cost_estimate=cost(2 * product, 8 * area),
        name="other_part",
    )(*near(other_grad, there, part), *far(query_rows), *near(key_state))

    given = lax.all_to_all(sent, "ctx", 0, 0, axis_index_groups=[order])

    def inner(base, number, after, near_rows):
        shapes, specs = [], []
        for top in near_rows:
            shapes.append(pltpu.VMEM((top, number * HEAD), BF16) if top else pltpu.HBM((length, number * HEAD), BF16))
            specs.append(IN_VMEM if top else pl.BlockSpec((length, PAIR), lambda h: (0, h)))
        if 0 < near_rows[2] < length:
            shapes.append(pltpu.HBM((length - near_rows[2], number * HEAD), BF16))
            specs.append(pl.BlockSpec((length - near_rows[2], PAIR), lambda h: (0, h)))
        return pl.pallas_call(
            functools.partial(inner_kernel, factor),
            grid=(number // 2,),
            in_specs=[ANYWHERE] + [pl.BlockSpec((length, PAIR), lambda h: (0, h + base // 2))] * 4,
            out_specs=specs,
            out_shape=shapes,
            scratch_shapes=[pltpu.VMEM((length // BLOCK, PAIR, PAIR), BF16)] * 2,
            compiler_params=params,
            cost_estimate=cost(6 * product * number / heads, 10 * area),
            name=f"inner_{base}",
        )(after, *far(query_rows, key_rows, value_rows, head_grad))

    half = heads // 2
    local_a = inner(0, half, key_state, (0, 0, 0))
    carried = pl.pallas_call(
        functools.partial(middle_kernel, factor, place),
        in_specs=[IN_VMEM, ANYWHERE],
        out_specs=IN_VMEM,
        out_shape=pltpu.VMEM(given.shape, BF16),
        compiler_params=pltpu.CompilerParams(vmem_limit_bytes=4 * MIB),
        name="sums",
    )(*near(given), *far(local_a[0]))
    local_b = inner(half, heads - half, carried, (length, length, length - TILE // 2))
    carried = lax.all_to_all(carried, "ctx", 0, 0, axis_index_groups=[order])

    full, part_width = pltpu.VMEM((length, width), BF16), pltpu.VMEM((length, width // 2), BF16)
    tail = pltpu.VMEM((TILE // 2, width // 2), BF16)
    steps = tiles + 1
    return pl.pallas_call(
        last_kernel,
        in_specs=[IN_VMEM] + [ANYWHERE] * 6 + [IN_VMEM] * 3 + [ANYWHERE],
        out_specs=[ANYWHERE] * 3,
        out_shape=[jax.ShapeDtypeStruct((length, width), BF16)] * 3,
        scratch_shapes=[full, part_width, full, part_width, full, part_width, tail, full, full, full]
        + [semaphores((7, steps)), semaphores((3, steps))],
        compiler_params=pltpu.CompilerParams(vmem_limit_bytes=24 * MIB),
        cost_estimate=cost(product, 18 * area),
        name="carried_part",
    )(*near(carried), *far(key_rows, value_rows, head_grad, *local_a), *near(*local_b[:3]), *far(local_b[3]))


def solution(mesh):
    rows = P("ctx", "head")
    return jax.shard_map(
        per_device,
        mesh=mesh,
        in_specs=(rows, rows, rows, rows, P("head", None)),
        out_specs=(rows, rows, rows),
        check_vma=False,
    )
```
